128 devices in a mesh: dom: 128 (over y, z, x, core).
Axes of the slice: x: 4, y: 4, z: 4, core: 2. Of those that a mesh axis runs over, the one named last changes fastest.
Arguments:
- features: bfloat16 [524288, 128], P('dom'), may hold values from -6 to 6
- cotangent: bfloat16 [524288, 128], P('dom'), may hold values from -6 to 6
- weights: bfloat16 [4, 128, 128], replicated, may hold values from -0.5 to 0.5
- fine_tiles: bfloat16 [4096, 12, 128, 128], P('dom'), may hold values from -0.15625 to 0.15625
- fine_columns: int32 [128, 32, 12], P('dom'), may hold values from 0 to 39, as said below
- fine_halo: int32 [128, 4, 256], P('dom'), may hold values from 0 to 4095
- coarse_tiles: bfloat16 [2560, 12, 128, 128], P('dom'), may hold values from -0.15625 to 0.15625
- coarse_columns: int32 [128, 20, 12], P('dom'), may hold values from 0 to 27, as said below
- coarse_halo: int32 [128, 4, 256], P('dom'), may hold values from 0 to 2559, as said below
- pair_send: int32 [128, 4, 256], P('dom'), may hold values from 0 to 4095, as said below
- members: int32 [128, 2, 2560], P('dom'), may hold values from 0 to 5119, as said below
- coarse_count: int32 [128], P('dom'), may hold values from 1536 to 2560
Outputs:
- result: bfloat16 [524288, 128], P('dom')
- grad_features: bfloat16 [524288, 128], P('dom')
- grad_weights: float32 [4, 128, 128], replicated
The draws below stay inside these ranges and needn't reach their ends.
Inputs may be any that keep to these rules, and one draw needn't show every extreme that they name: `fine_columns`: entry 0 of row block b is b itself and entry 1 is halo block 32 + (b mod 8). `coarse_columns`: entry 0 of row block b is b itself and entry 1 is halo block 20 + (b mod 8). `coarse_halo`: entries of partition p are below coarse_count[p]; in direction 0 the first entry is coarse_count[p] - 1 and the second is 0. `pair_send`: the 1024 entries of one partition are different rows. `members`: A live cell names two different rows; dead cells name row 0 twice. Every fine row belongs to exactly one live cell, of its own partition or of the neighbour that receives it.
All inputs are finite; a program needn't handle non-finite values.
Results may differ from the reference program's by a relative error of at most 0.013.
Values may be sent and summed in bfloat16 or wider, within the bound.
A program may use at most 192 MiB of HBM per device.

```python
import jax
import jax.numpy as jnp
from jax import lax

H = 128
TILE = 128
KT = 12
NODE_DEV = 4096
HALO = 256
PAIR = 256
NC_DEV = 2560
NODES = 524288
N_DOM = 128


OFFSETS = (1, -1, 8, -8)


def pairing(key):
    subkeys = jax.random.split(jax.random.fold_in(key, 7001), 3)
    counts = 2 * jax.random.randint(subkeys[0], (N_DOM, 4), 0, PAIR // 2 + 1)
    for index in range(4):
        sender = (16 - OFFSETS[index]) % N_DOM
        counts = counts.at[sender, index].set(PAIR)
    counts = counts.at[0].set(PAIR)
    counts = counts.at[16].set(0)
    ordering = jax.vmap(lambda inner: jax.random.permutation(inner, NODE_DEV))(jax.random.split(subkeys[1], N_DOM)).astype(jnp.int32)
    position = jnp.arange(NODE_DEV, dtype=jnp.int32)
    direction = jnp.minimum(position // PAIR, 3)
    outgoing = (position < 4 * PAIR)[None, :] & ((position % PAIR)[None, :] < counts[:, direction])
    local_pos = jnp.argsort(outgoing.astype(jnp.int32), axis=1, stable=True)
    local_rows = jnp.take_along_axis(ordering, local_pos, axis=1)
    incoming_counts = jnp.stack([jnp.roll(counts[:, index], OFFSETS[index]) for index in range(4)], axis=1)
    slot_index = jnp.arange(4 * PAIR, dtype=jnp.int32)
    valid_in = (slot_index % PAIR)[None, :] < incoming_counts[:, slot_index // PAIR]
    in_pos = jnp.argsort(1 - valid_in.astype(jnp.int32), axis=1, stable=True).astype(jnp.int32)
    sent_total = counts.sum(axis=1)
    got_total = incoming_counts.sum(axis=1)
    live_count = got_total + (NODE_DEV - sent_total - got_total) // 2
    cell_index = jnp.broadcast_to(jnp.arange(NC_DEV, dtype=jnp.int32)[None, :], (N_DOM, NC_DEV))
    incoming_cell = cell_index < got_total[:, None]
    local_step = cell_index - got_total[:, None]
    first_idx = jnp.where(incoming_cell, cell_index, got_total[:, None] + 2 * local_step)
    first_idx = jnp.clip(first_idx, 0, NODE_DEV - 1)
    second_idx = jnp.clip(got_total[:, None] + 2 * local_step + 1, 0, NODE_DEV - 1)
    in_idx = jnp.clip(cell_index, 0, 4 * PAIR - 1)
    first_member = jnp.take_along_axis(local_rows, first_idx, axis=1)
    second = jnp.where(incoming_cell, NODE_DEV + jnp.take_along_axis(in_pos, in_idx, axis=1), jnp.take_along_axis(local_rows, second_idx, axis=1))
    alive = cell_index < live_count[:, None]
    first_member = jnp.where(alive, first_member, 0)
    second = jnp.where(alive, second, 0)
    scores = jax.vmap(lambda inner: jax.random.permutation(inner, NC_DEV))(jax.random.split(subkeys[2], N_DOM)).astype(jnp.int32)
    scores = jnp.where(alive, scores, NC_DEV + cell_index)
    shuffle = jnp.argsort(scores, axis=1, stable=True)
    first_member = jnp.take_along_axis(first_member, shuffle, axis=1)
    second = jnp.take_along_axis(second, shuffle, axis=1)
    send_rows = ordering[:, :4 * PAIR].reshape(N_DOM, 4, PAIR)
    return (send_rows, jnp.stack([first_member, second], axis=1).astype(jnp.int32), live_count.astype(jnp.int32))


def block_columns(key, blocks):
    halo_blocks = 4 * HALO // TILE
    others = jax.random.randint(key, (N_DOM, blocks, KT - 2), 0, blocks + halo_blocks)
    own_block = jnp.broadcast_to(jnp.arange(blocks, dtype=jnp.int32)[None, :], (N_DOM, blocks))
    halo_block = blocks + own_block % halo_blocks
    return jnp.concatenate([own_block[:, :, None], halo_block[:, :, None], others], axis=2).astype(jnp.int32)


def draw_fine_columns(key, part):
    key = jax.random.fold_in(key, 11)
    return block_columns(key, NODE_DEV // TILE)


def draw_coarse_columns(key, part):
    key = jax.random.fold_in(key, 12)
    return block_columns(key, NC_DEV // TILE)


def draw_pair_send(key, part):
    shared = pairing(key)
    return shared[0]


def draw_members(key, part):
    shared = pairing(key)
    return shared[1]


def draw_coarse_count(key, part):
    shared = pairing(key)
    return shared[2]


def draw_coarse_halo(key, part):
    shared = pairing(key)
    key = jax.random.fold_in(key, 41)
    live = shared[2]
    picked = jax.random.randint(key, (N_DOM, 4, HALO), 0, live[:, None, None]).astype(jnp.int32)
    picked = picked.at[:, 0, 0].set(live - 1)
    picked = picked.at[:, 0, 1].set(0)
    return picked.astype(jnp.int32)


def plant(values, key, least, top_value):
    longest = values.shape.index(max(values.shape))
    spots = []
    for shift in (0, 1):
        where = [jax.random.randint(jax.random.fold_in(key, axis), (), 0, length) for axis, length in enumerate(values.shape)]
        where[longest] = (where[longest] + shift) % values.shape[longest]
        spots.append(tuple(where))
    return values.at[spots[0]].set(least).at[spots[1]].set(top_value)


def shard_levels(key, shape, cuts, least, top_value):
    factor_of = 1.0
    for axis_at, blocks in cuts:
        steps = jax.random.uniform(jax.random.fold_in(jax.random.fold_in(key, 6), axis_at), (blocks,), jnp.float32, least / len(cuts), top_value / len(cuts))
        factor_of = factor_of * jnp.repeat(jnp.exp(steps), shape[axis_at] // blocks).reshape((-1,) + (1,) * (len(shape) - 1 - axis_at))
    return factor_of


def normal_values(key, extent, deviation, reach, cuts=(), held_as=jnp.bfloat16):
    values = jax.random.normal(key, extent, jnp.float32) * deviation
    if len(cuts) > 0:
        values = shard_levels(key, extent, cuts, -0.22, 0.18) * values
    return jnp.clip(values, min=-reach, max=reach).astype(held_as)


def setup_inputs(seed: int = 0) -> dict:
    key_list = jax.random.split(jax.random.key(seed), 13)
    return {
        "features": normal_values(key_list[0], (NODES, H), 1.0, 6.0, ((0, 128),)),
        "cotangent": normal_values(key_list[1], (NODES, H), 1.0, 6.0, ((0, 128),)),
        "weights": normal_values(key_list[2], (4, H, H), H ** -0.5, 0.5),
        "fine_tiles": normal_values(key_list[3], (N_DOM * NODE_DEV // TILE, KT, TILE, TILE), (KT * TILE) ** -0.5, 0.15625, ((0, 128),)),
        "fine_columns": draw_fine_columns(jax.random.fold_in(key_list[12], 71), 0),
        "fine_halo": plant(jax.random.randint(key_list[5], (N_DOM, 4, HALO), 0, NODE_DEV), jax.random.fold_in(key_list[5], 1), 0, NODE_DEV - 1).astype(jnp.int32),
        "coarse_tiles": normal_values(key_list[6], (N_DOM * NC_DEV // TILE, KT, TILE, TILE), (KT * TILE) ** -0.5, 0.15625, ((0, 128),)),
        "coarse_columns": draw_coarse_columns(jax.random.fold_in(key_list[12], 71), 0),
        "coarse_halo": draw_coarse_halo(jax.random.fold_in(key_list[12], 71), 0),
        "pair_send": draw_pair_send(jax.random.fold_in(key_list[12], 71), 0),
        "members": draw_members(jax.random.fold_in(key_list[12], 71), 0),
        "coarse_count": draw_coarse_count(jax.random.fold_in(key_list[12], 71), 0),
    }


OFFSETS = (1, -1, 8, -8)

def silu_grad(value):
    sigma = jax.nn.sigmoid(value)
    return sigma * (1.0 + value * (1.0 - sigma))

def extend(values, send_rows):
    pieces = [values]
    for index in range(4):
        picked = jax.vmap(lambda rows, where: rows[where])(values, send_rows[:, index])
        pieces.append(jnp.roll(picked, OFFSETS[index], axis=0))
    return jnp.concatenate(pieces, axis=1)

def retract(grad_ext, send_rows, row_count, halo_rows):
    own_rows = grad_ext[:, :row_count]
    for index in range(4):
        piece = grad_ext[:, row_count + index * halo_rows:row_count + (index + 1) * halo_rows]
        moved = jnp.roll(piece, -OFFSETS[index], axis=0)
        own_rows = jax.vmap(lambda target, where, added: target.at[where].add(added))(own_rows, send_rows[:, index], moved)
    return own_rows

def aggregate(tile_values, columns, extended):
    blocks = extended.reshape(-1, TILE, H)[columns]
    summed = jnp.einsum('bktu,bkuh->bth', tile_values.astype(jnp.float32), blocks.astype(jnp.float32))
    return summed.reshape(-1, H)

def spread(tile_values, columns, gradient, block_count):
    partial_value = jnp.einsum('bktu,bth->bkuh', tile_values.astype(jnp.float32), gradient.reshape(tile_values.shape[0], TILE, H).astype(jnp.float32))
    summed_rows = jnp.zeros((block_count, TILE, H), jnp.float32).at[columns.reshape(-1)].add(partial_value.reshape(-1, TILE, H))
    return summed_rows.reshape(block_count * TILE, H)

def level_forward(values, message_weight, update_weight, tile_values, columns, send_rows):
    shape = values.shape
    messages = jnp.dot(values.reshape(-1, H), message_weight, preferred_element_type=jnp.float32).astype(jnp.bfloat16).reshape(shape)
    extended = extend(messages, send_rows)
    summed = lax.map(lambda operands: aggregate(*operands), (tile_values, columns, extended))
    gated_rows = jax.nn.silu(summed).astype(jnp.bfloat16)
    update = jnp.dot(gated_rows.reshape(-1, H), update_weight, preferred_element_type=jnp.float32).reshape(shape)
    return ((values.astype(jnp.float32) + update).astype(jnp.bfloat16), summed, gated_rows)

def level_backward(values, summed, gated_rows, grad_out, message_weight, update_weight, tile_values, columns, send_rows):
    shape = values.shape
    row_count = shape[1]
    halo_rows = send_rows.shape[2]
    block_count = (row_count + 4 * halo_rows) // TILE
    grad_low = grad_out.astype(jnp.bfloat16).reshape(-1, H)
    grad_update = jnp.dot(gated_rows.reshape(-1, H).T, grad_low, preferred_element_type=jnp.float32)
    grad_gated = jnp.dot(grad_low, update_weight.T, preferred_element_type=jnp.float32).reshape(shape)
    grad_summed = (grad_gated * silu_grad(summed)).astype(jnp.bfloat16)
    grad_ext = lax.map(lambda operands: spread(operands[0], operands[1], operands[2], block_count), (tile_values, columns, grad_summed))
    grad_msg = retract(grad_ext, send_rows, row_count, halo_rows)
    msg_low = grad_msg.astype(jnp.bfloat16).reshape(-1, H)
    grad_message = jnp.dot(values.reshape(-1, H).T, msg_low, preferred_element_type=jnp.float32)
    grad_values = grad_out + jnp.dot(msg_low, message_weight.T, preferred_element_type=jnp.float32).reshape(shape)
    return (grad_values, grad_message, grad_update)

def pool_rows(values, send_rows, members, alive_mask):
    extended = extend(values, send_rows)
    picked = jax.vmap(lambda rows, pair_index: rows[pair_index[0]].astype(jnp.float32) + rows[pair_index[1]].astype(jnp.float32))(extended, members)
    return jnp.where(alive_mask[:, :, None], picked, jnp.float32(0.0))

def unpool(values, send_rows, members, alive_mask):
    masked = jnp.where(alive_mask[:, :, None], values, jnp.float32(0.0))

    def place_rows(pair_index, added):
        table = jnp.zeros((NODE_DEV + 4 * PAIR, H), jnp.float32)
        return table.at[pair_index[0]].add(added).at[pair_index[1]].add(added)
    extended = jax.vmap(place_rows)(members, masked)
    return retract(extended, send_rows, NODE_DEV, PAIR)

def reference(features, cotangent, weights, fine_tiles, fine_columns, fine_halo, coarse_tiles, coarse_columns, coarse_halo, pair_send, members, coarse_count):
    fine_parts = features.reshape(N_DOM, NODE_DEV, H)
    cot_parts = cotangent.reshape(N_DOM, NODE_DEV, H)
    fine_tile_parts = fine_tiles.reshape(N_DOM, NODE_DEV // TILE, KT, TILE, TILE)
    coarse_tile_parts = coarse_tiles.reshape(N_DOM, NC_DEV // TILE, KT, TILE, TILE)
    alive_mask = jnp.arange(NC_DEV, dtype=jnp.int32)[None, :] < coarse_count[:, None]
    fine_out, fine_summed, fine_gated = level_forward(fine_parts, weights[0], weights[1], fine_tile_parts, fine_columns, fine_halo)
    coarse_in = pool_rows(fine_out, pair_send, members, alive_mask).astype(jnp.bfloat16)
    coarse_out, coarse_summed, coarse_gated = level_forward(coarse_in, weights[2], weights[3], coarse_tile_parts, coarse_columns, coarse_halo)
    result = (fine_out.astype(jnp.float32) + unpool(coarse_out.astype(jnp.float32), pair_send, members, alive_mask)).astype(jnp.bfloat16)
    grad_coarse_out = pool_rows(cot_parts, pair_send, members, alive_mask)
    grad_coarse_in, grad_two, grad_three = level_backward(coarse_in, coarse_summed, coarse_gated, grad_coarse_out, weights[2], weights[3], coarse_tile_parts, coarse_columns, coarse_halo)
    grad_fine_out = cot_parts.astype(jnp.float32) + unpool(grad_coarse_in, pair_send, members, alive_mask)
    grad_input, grad_zero, grad_one = level_backward(fine_parts, fine_summed, fine_gated, grad_fine_out, weights[0], weights[1], fine_tile_parts, fine_columns, fine_halo)
    grad_stack = jnp.stack([grad_zero, grad_one, grad_two, grad_three])
    return (result.reshape(NODES, H), grad_input.astype(jnp.bfloat16).reshape(NODES, H), grad_stack)
```

```python
import functools

import jax
import jax.numpy as jnp
from jax import lax
from jax.experimental import pallas as pl
from jax.experimental.pallas import tpu as pltpu
from jax.sharding import PartitionSpec as P

MESH = pl.DeviceIdType.MESH
OFFSETS = (1, -1, 8, -8)
F32, BF16, I32 = jnp.float32, jnp.bfloat16, jnp.int32
VMEM = pl.BlockSpec(memory_space=pltpu.VMEM)
SMEM = pl.BlockSpec(memory_space=pltpu.SMEM)
ANY = pl.BlockSpec(memory_space=pl.ANY)
DMA = pltpu.SemaphoreType.DMA
H = 128
T = 128
KT = 12
FB = 32
CB = 20
NF = FB * T
NC = CB * T
SEND = 256
HALO = 4 * SEND
QUAD = 4 * T
UNROLL = 16
NN = (((1,), (0,)), ((), ()))
NT = (((1,), (1,)), ((), ()))
TN = (((0,), (0,)), ((), ()))


def dot(a, b, how=NN):
    return lax.dot_general(a, b, how, preferred_element_type=F32)


def shape(dims, dtype):
    return jax.ShapeDtypeStruct(dims, dtype)


def params(mib=56, **more):
    return pltpu.CompilerParams(vmem_limit_bytes=mib * 2**20, **more)


def neighbour(me, n, offset):
    return lax.rem(me + (offset + n), n)


def greet(me, n):
    barrier = pltpu.get_barrier_semaphore()
    for offset in OFFSETS:
        pl.semaphore_signal(
            barrier, inc=1, device_id=(neighbour(me, n, offset),), device_id_type=MESH
        )
    return barrier


def remote(src, dst, send_sem, recv_sem, target):
    return pltpu.make_async_remote_copy(
        src_ref=src,
        dst_ref=dst,
        send_sem=send_sem,
        recv_sem=recv_sem,
        device_id=(target,),
        device_id_type=MESH,
    )


def index_copies(pairs, sem):
    copies = []
    for src, dst in pairs:
        width = src.shape[2]
        for j in range(src.shape[1]):
            copies.append((src.at[0, j], dst.at[pl.ds(j * width, width)]))
    return [pltpu.make_async_copy(a, b, sem.at[i]) for i, (a, b) in enumerate(copies)]


def loop(count, body, unroll=1):
    def step(i, carry):
        body(i)
        return carry

    lax.fori_loop(0, count, step, 0, unroll=unroll)


def gather_rows(index, first, source, target, count, width=1):
    def body(i):
        base = pl.multiple_of(i * UNROLL, UNROLL)
        rows = [
            source[pl.ds(index[first + base + u] * width, width), :]
            for u in range(UNROLL)
        ]
        for u in range(UNROLL):
            target[pl.ds((base + u) * width, width), :] = rows[u]

    loop(count // UNROLL, body)


def block_row(tiles, columns, blocks, b, first):
    lhs = jnp.concatenate([tiles[b, k] for k in range(KT)], axis=1)
    rhs = jnp.concatenate([blocks[columns[first + k]] for k in range(KT)], axis=0)
    return dot(lhs, rhs)


def spread_row(tiles, columns, grads_t, b, first, total):
    for k in range(KT):
        c = columns[first + k]
        total[c] = total[c] + dot(grads_t, tiles[b, k])


def tile_copies(source, buffer, sem, count):
    size = source.shape[0] // count
    return [
        pltpu.make_async_copy(
            source.at[pl.ds(i * size, size)], buffer.at[pl.ds(i * size, size)], sem.at[i]
        )
        for i in range(count)
    ]


def wait_tiles(source, buffer, sem, i, size):
    pltpu.make_async_copy(
        source.at[pl.ds(i * size, size)], buffer.at[pl.ds(i * size, size)], sem.at[i]
    ).wait()


def forward_kernel(
    n,
    values,
    cot,
    weights,
    columns,
    count,
    fine_halo,
    coarse_halo,
    pair_send,
    members,
    tiles,
    h1_out,
    gate_out,
    slope_out,
    own_out,
    halo_out,
    z0_out,
    dz1_out,
    buf,
    ext,
    rows32,
    pairs,
    cells,
    stage,
    send_fine,
    send_pair,
    recv_pair,
    send_coarse,
    recv_coarse,
    s_fine,
    s_coarse,
    s_pair,
    s_members,
    tile_sem,
    index_sem,
    send_sem,
    recv_sem,
):
    me = lax.axis_index("dom")
    barrier = greet(me, n)
    index = index_copies(
        [(fine_halo, s_fine), (coarse_halo, s_coarse), (pair_send, s_pair), (members, s_members)],
        index_sem,
    )
    for copy in index:
        copy.start()
    for copy in tile_copies(tiles, buf, tile_sem, 8):
        copy.start()

    def project(i):
        at = pl.ds(i * QUAD, QUAD)
        low = dot(values[at, :], weights[0]).astype(BF16)
        rows32[at, :] = low.astype(F32)
        ext[pl.ds(i * 4, 4)] = low.reshape(4, T, H)

    loop(NF // QUAD, project)
    for copy in index:
        copy.wait()
    pl.semaphore_wait(barrier, 4)

    targets = [neighbour(me, n, offset) for offset in OFFSETS]
    fine = []
    for j in range(4):
        gather_rows(s_fine, j * SEND, rows32, stage, SEND)
        send_fine[pl.ds(2 * j, 2)] = stage[:SEND, :].astype(BF16).reshape(2, T, H)
        copy = remote(
            send_fine.at[pl.ds(2 * j, 2)],
            ext.at[pl.ds(FB + 2 * j, 2)],
            send_sem.at[j],
            recv_sem.at[j],
            targets[j],
        )
        copy.start()
        fine.append(copy)

    def place_cot(i):
        pairs[pl.ds(i * 2 * QUAD + 1, QUAD, stride=2), :] = cot[pl.ds(i * QUAD, QUAD), :].astype(F32)

    loop(NF // QUAD, place_cot)
    for copy in fine:
        copy.wait()

    def level(i):
        wait_tiles(tiles, buf, tile_sem, i, 4)
        parts = []
        for q in range(4):
            b = i * 4 + q
            parts.append(block_row(buf, columns, ext, b, b * KT))
        summed = jnp.concatenate(parts, axis=0)
        sigma = jax.nn.sigmoid(summed)
        gate = (summed * sigma).astype(BF16)
        at = pl.ds(i * QUAD, QUAD)
        gate_out[at, :] = gate
        slope_out[at, :] = (sigma * (1.0 + summed * (1.0 - sigma))).astype(BF16)
        out = (values[at, :].astype(F32) + dot(gate, weights[1])).astype(BF16)
        h1_out[at, :] = out
        pairs[pl.ds(i * 2 * QUAD, QUAD, stride=2), :] = out.astype(F32)

    loop(8, level)

    paired = []
    for j in range(4):
        gather_rows(s_pair, j * SEND, pairs, stage, SEND, 2)
        send_pair[j] = stage[...].astype(BF16)
        copy = remote(
            send_pair.at[j], recv_pair.at[j], send_sem.at[4 + j], recv_sem.at[4 + j], targets[j]
        )
        copy.start()
        paired.append(copy)
    for j in range(4):
        paired[j].wait()
        pairs[pl.ds(2 * NF + j * 2 * SEND, 2 * SEND), :] = recv_pair[j].astype(F32)

    def pool(i):
        base = pl.multiple_of(i * UNROLL, UNROLL)
        first = [pairs[pl.ds(s_members[base + u] * 2, 2), :] for u in range(UNROLL)]
        second = [pairs[pl.ds(s_members[NC + base + u] * 2, 2), :] for u in range(UNROLL)]
        for u in range(UNROLL):
            cells[pl.ds((base + u) * 2, 2), :] = first[u] + second[u]

    loop(NC // UNROLL, pool)
    live = count[0]

    def pooled(i):
        at = pl.ds(i * QUAD, QUAD)
        row = lax.broadcasted_iota(I32, (QUAD, H), 0) + i * QUAD
        alive = row < live
        z0 = jnp.where(alive, cells[pl.ds(i * 2 * QUAD, QUAD, stride=2), :], 0.0).astype(BF16)
        z0_out[at, :] = z0
        dz1_out[at, :] = jnp.where(
            alive, cells[pl.ds(i * 2 * QUAD + 1, QUAD, stride=2), :], 0.0
        ).astype(BF16)
        low = dot(z0, weights[2]).astype(BF16)
        rows32[at, :] = low.astype(F32)
        own_out[pl.ds(i * 4, 4)] = low.reshape(4, T, H)

    loop(NC // QUAD, pooled)
    coarse = []
    for j in range(4):
        gather_rows(s_coarse, j * SEND, rows32, stage, SEND)
        send_coarse[pl.ds(2 * j, 2)] = stage[:SEND, :].astype(BF16).reshape(2, T, H)
        copy = remote(
            send_coarse.at[pl.ds(2 * j, 2)],
            recv_coarse.at[pl.ds(2 * j, 2)],
            send_sem.at[8 + j],
            recv_sem.at[8 + j],
            targets[j],
        )
        copy.start()
        coarse.append(copy)
    for copy in coarse:
        copy.wait()
    halo_out[...] = recv_coarse[...]


def forward(n, values, cot, weights, columns, count, fine_halo, coarse_halo, pair_send, members, tiles):
    return pl.pallas_call(
        functools.partial(forward_kernel, n),
        name="forward",
        out_shape=[
            shape((NF, H), BF16),
            shape((NF, H), BF16),
            shape((NF, H), BF16),
            shape((CB, T, H), BF16),
            shape((8, T, H), BF16),
            shape((NC, H), BF16),
            shape((NC, H), BF16),
        ],
        in_specs=[VMEM, VMEM, VMEM, SMEM, SMEM, ANY, ANY, ANY, ANY, ANY],
        out_specs=[VMEM] * 7,
        scratch_shapes=[
            pltpu.VMEM((FB, KT, T, T), BF16),
            pltpu.VMEM((FB + 8, T, H), BF16),
            pltpu.VMEM((NF, H), F32),
            pltpu.VMEM((2 * (NF + HALO), H), F32),
            pltpu.VMEM((2 * NC, H), F32),
            pltpu.VMEM((2 * SEND, H), F32),
            pltpu.VMEM((8, T, H), BF16),
            pltpu.VMEM((4, 2 * SEND, H), BF16),
            pltpu.VMEM((4, 2 * SEND, H), BF16),
            pltpu.VMEM((8, T, H), BF16),
            pltpu.VMEM((8, T, H), BF16),
            pltpu.SMEM((HALO,), I32),
            pltpu.SMEM((HALO,), I32),
            pltpu.SMEM((HALO,), I32),
            pltpu.SMEM((2 * NC,), I32),
            DMA((8,)),
            DMA((14,)),
            DMA((12,)),
            DMA((12,)),
        ],
        compiler_params=params(collective_id=0, has_side_effects=True),
    )(values, cot, weights, columns, count, fine_halo, coarse_halo, pair_send, members, tiles)


def rows_out(total, blocks, own_ref, halo_ref):
    def own(c):
        own_ref[pl.ds(c * T, T), :] = jnp.transpose(total[c])

    loop(blocks, own, 4)

    def halo(c):
        halo_ref[pl.ds(c * T, T), :] = jnp.transpose(total[blocks + c]).astype(BF16)

    loop(8, halo, 4)


def coarse_kernel(
    own,
    halo,
    z0,
    dz1,
    weights,
    columns,
    tiles,
    z1_out,
    dm_out,
    piece_out,
    update_out,
    buf,
    ext,
    gates,
    total,
    tile_sem,
):
    for copy in tile_copies(tiles, buf, tile_sem, 5):
        copy.start()
    ext[pl.ds(0, CB)] = own[...]
    ext[pl.ds(CB, 8)] = halo[...]
    total[...] = jnp.zeros_like(total)

    def level(i):
        wait_tiles(tiles, buf, tile_sem, i, 4)
        parts = []
        for q in range(4):
            b = i * 4 + q
            parts.append(block_row(buf, columns, ext, b, b * KT))
        summed = jnp.concatenate(parts, axis=0)
        sigma = jax.nn.sigmoid(summed)
        gate = (summed * sigma).astype(BF16)
        at = pl.ds(i * QUAD, QUAD)
        gates[at, :] = gate
        z1_out[at, :] = (z0[at, :].astype(F32) + dot(gate, weights[3])).astype(BF16)
        slope = sigma * (1.0 + summed * (1.0 - sigma))
        grads = (dot(dz1[at, :], weights[3], NT) * slope).astype(BF16)
        for q in range(4):
            b = i * 4 + q
            grads_t = jnp.transpose(grads[q * T : (q + 1) * T, :])
            spread_row(buf, columns, grads_t, b, b * KT, total)

    loop(CB // 4, level)
    rows_out(total, CB, dm_out, piece_out)
    update_out[...] = dot(gates[...], dz1[...], TN)


def coarse_level(own, halo, z0, dz1, weights, columns, tiles):
    return pl.pallas_call(
        coarse_kernel,
        name="coarse_level",
        out_shape=[
            shape((NC, H), BF16),
            shape((NC, H), F32),
            shape((HALO, H), BF16),
            shape((H, H), F32),
        ],
        in_specs=[VMEM, VMEM, VMEM, VMEM, VMEM, SMEM, ANY],
        out_specs=[VMEM] * 4,
        scratch_shapes=[
            pltpu.VMEM((CB, KT, T, T), BF16),
            pltpu.VMEM((CB + 8, T, H), BF16),
            pltpu.VMEM((NC, H), BF16),
            pltpu.VMEM((CB + 8, T, H), F32),
            DMA((5,)),
        ],
        compiler_params=params(),
    )(own, halo, z0, dz1, weights, columns, tiles)


def swap_kernel(n, pieces, arrived, send_sem, recv_sem):
    me = lax.axis_index("dom")
    barrier = greet(me, n)
    pl.semaphore_wait(barrier, 4)
    size = pieces.shape[0] // 4
    copies = [
        remote(
            pieces.at[pl.ds(j * size, size)],
            arrived.at[pl.ds(j * size, size)],
            send_sem.at[j],
            recv_sem.at[j],
            neighbour(me, n, -OFFSETS[j]),
        )
        for j in range(4)
    ]
    for copy in copies:
        copy.start()
    for copy in copies:
        copy.wait()


def send_back(n, pieces, number):
    return pl.pallas_call(
        functools.partial(swap_kernel, n),
        name="send_back" + str(number),
        out_shape=shape(pieces.shape, pieces.dtype),
        in_specs=[ANY],
        out_specs=ANY,
        scratch_shapes=[DMA((4,)), DMA((4,))],
        compiler_params=params(1, collective_id=number, has_side_effects=True),
    )(pieces)


def add_rows(index, arrived, rows):
    def body(i):
        base = pl.multiple_of(i * UNROLL, UNROLL)
        for u in range(UNROLL):
            at = pl.ds(index[base + u], 1)
            rows[at, :] = rows[at, :] + arrived[pl.ds(base + u, 1), :]

    loop(HALO // UNROLL, body)


def coarse_back_kernel(
    dm,
    arrived,
    z0,
    dz1,
    z1,
    weights,
    count,
    coarse_halo,
    members,
    message_out,
    lifted_out,
    away_out,
    rows,
    add,
    cells,
    lifted,
    s_coarse,
    s_members,
    index_sem,
):
    index = index_copies([(coarse_halo, s_coarse), (members, s_members)], index_sem)
    for copy in index:
        copy.start()
    rows[...] = dm[...]
    add[...] = arrived[...].astype(F32)
    lifted[...] = jnp.zeros_like(lifted)
    for copy in index:
        copy.wait()
    add_rows(s_coarse, add, rows)
    low = rows[...].astype(BF16)
    message_out[...] = dot(z0[...], low, TN)

    def grads(i):
        at = pl.ds(i * QUAD, QUAD)
        cells[pl.ds(i * 2 * QUAD, QUAD, stride=2), :] = z1[at, :].astype(F32)
        cells[pl.ds(i * 2 * QUAD + 1, QUAD, stride=2), :] = dz1[at, :].astype(F32) + dot(
            rows[at, :].astype(BF16), weights[2], NT
        )

    loop(NC // QUAD, grads)
    live = count[0]

    def place(base, size):
        values = [cells[pl.ds((base + u) * 2, 2), :] for u in range(size)]
        for u in range(size):
            lifted[pl.ds(pl.multiple_of(s_members[base + u] * 2, 2), 2), :] = values[u]
            lifted[pl.ds(pl.multiple_of(s_members[NC + base + u] * 2, 2), 2), :] = values[u]

    groups = live // UNROLL
    loop(groups, lambda i: place(pl.multiple_of(i * UNROLL, UNROLL), UNROLL))
    loop(live - groups * UNROLL, lambda i: place(groups * UNROLL + i, 1))
    lifted_out[...] = lifted[: 2 * NF, :].astype(BF16)
    away_out[...] = lifted[2 * NF :, :].astype(BF16)


def coarse_back(dm, arrived, z0, dz1, z1, weights, count, coarse_halo, members):
    return pl.pallas_call(
        coarse_back_kernel,
        name="coarse_back",
        out_shape=[shape((H, H), F32), shape((2 * NF, H), BF16), shape((2 * HALO, H), BF16)],
        in_specs=[VMEM] * 6 + [SMEM, ANY, ANY],
        out_specs=[VMEM] * 3,
        scratch_shapes=[
            pltpu.VMEM((NC, H), F32),
            pltpu.VMEM((HALO, H), F32),
            pltpu.VMEM((2 * NC, H), F32),
            pltpu.VMEM((2 * (NF + HALO), H), F32),
            pltpu.SMEM((HALO,), I32),
            pltpu.SMEM((2 * NC,), I32),
            DMA((6,)),
        ],
        compiler_params=params(),
    )(dm, arrived, z0, dz1, z1, weights, count, coarse_halo, members)


def fine_kernel(
    lifted,
    returned,
    h1,
    cot,
    gate,
    slope,
    weights,
    columns,
    pair_send,
    tiles,
    result_out,
    low_out,
    dm_out,
    piece_out,
    update_out,
    buf,
    pairs,
    add,
    total,
    s_pair,
    index_sem,
    tile_sem,
):
    index = index_copies([(pair_send, s_pair)], index_sem)
    for copy in index:
        copy.start()
    for copy in tile_copies(tiles, buf, tile_sem, 8):
        copy.start()
    pairs[...] = lifted[...].astype(F32)
    add[...] = returned[...].astype(F32)
    total[...] = jnp.zeros_like(total)
    update_out[...] = jnp.zeros_like(update_out)
    for copy in index:
        copy.wait()

    def place(i):
        base = pl.multiple_of(i * UNROLL, UNROLL)
        at = [pl.ds(pl.multiple_of(s_pair[base + u] * 2, 2), 2) for u in range(UNROLL)]
        values = [pairs[at[u], :] + add[pl.ds((base + u) * 2, 2), :] for u in range(UNROLL)]
        for u in range(UNROLL):
            pairs[at[u], :] = values[u]

    loop(HALO // UNROLL, place)

    def level(i):
        at = pl.ds(i * QUAD, QUAD)
        result_out[at, :] = (
            h1[at, :].astype(F32) + pairs[pl.ds(i * 2 * QUAD, QUAD, stride=2), :]
        ).astype(BF16)
        low = (
            cot[at, :].astype(F32) + pairs[pl.ds(i * 2 * QUAD + 1, QUAD, stride=2), :]
        ).astype(BF16)
        low_out[at, :] = low
        update_out[...] += dot(gate[at, :], low, TN)
        grads = (dot(low, weights[1], NT) * slope[at, :].astype(F32)).astype(BF16)
        wait_tiles(tiles, buf, tile_sem, i, 4)
        for q in range(4):
            b = i * 4 + q
            grads_t = jnp.transpose(grads[q * T : (q + 1) * T, :])
            spread_row(buf, columns, grads_t, b, b * KT, total)

    loop(8, level)
    rows_out(total, FB, dm_out, piece_out)


def fine_level(lifted, returned, h1, cot, gate, slope, weights, columns, pair_send, tiles):
    return pl.pallas_call(
        fine_kernel,
        name="fine_level",
        out_shape=[
            shape((NF, H), BF16),
            shape((NF, H), BF16),
            shape((NF, H), F32),
            shape((HALO, H), BF16),
            shape((H, H), F32),
        ],
        in_specs=[VMEM] * 7 + [SMEM, ANY, ANY],
        out_specs=[VMEM] * 5,
        scratch_shapes=[
            pltpu.VMEM((FB, KT, T, T), BF16),
            pltpu.VMEM((2 * NF, H), F32),
            pltpu.VMEM((2 * HALO, H), F32),
            pltpu.VMEM((FB + 8, T, H), F32),
            pltpu.SMEM((HALO,), I32),
            DMA((4,)),
            DMA((8,)),
        ],
        compiler_params=params(),
    )(lifted, returned, h1, cot, gate, slope, weights, columns, pair_send, tiles)


def fine_back_kernel(
    dm, arrived, values, low, weights, fine_halo, grad_out, message_out, rows, add, s_fine, index_sem
):
    index = index_copies([(fine_halo, s_fine)], index_sem)
    for copy in index:
        copy.start()
    rows[...] = dm[...]
    add[...] = arrived[...].astype(F32)
    message_out[...] = jnp.zeros_like(message_out)
    for copy in index:
        copy.wait()
    add_rows(s_fine, add, rows)

    def grads(i):
        at = pl.ds(i * QUAD, QUAD)
        part = rows[at, :].astype(BF16)
        message_out[...] += dot(values[at, :], part, TN)
        grad_out[at, :] = (low[at, :].astype(F32) + dot(part, weights[0], NT)).astype(BF16)

    loop(8, grads)


def fine_back(dm, arrived, values, low, weights, fine_halo):
    return pl.pallas_call(
        fine_back_kernel,
        name="fine_back",
        out_shape=[shape((NF, H), BF16), shape((H, H), F32)],
        in_specs=[VMEM] * 5 + [ANY],
        out_specs=[VMEM] * 2,
        scratch_shapes=[
            pltpu.VMEM((NF, H), F32),
            pltpu.VMEM((HALO, H), F32),
            pltpu.SMEM((HALO,), I32),
            DMA((4,)),
        ],
        compiler_params=params(),
    )(dm, arrived, values, low, weights, fine_halo)


NEAR = 8
FAR = 16


def total_kernel(
    n,
    m0,
    u0,
    m1,
    u1,
    out_ref,
    grads,
    near,
    part,
    far,
    whole,
    sum_send,
    sum_recv,
    far_send,
    far_recv,
    all_send,
    all_recv,
):
    me = lax.axis_index("dom")
    group, rank = me // NEAR, me % NEAR
    close = [group * NEAR + (rank + s) % NEAR for s in range(1, NEAR)]
    distant = [((group + s) % FAR) * NEAR + rank for s in range(1, FAR)]
    barrier = pltpu.get_barrier_semaphore()
    for target in close + distant:
        pl.semaphore_signal(barrier, inc=1, device_id=(target,), device_id_type=MESH)
    for i, ref in enumerate((m0, u0, m1, u1)):
        grads[pl.ds(i * H, H), :] = ref[...]
    pl.semaphore_wait(barrier, NEAR - 1 + FAR - 1)
    size = 4 * H // NEAR
    copies = []
    for s in range(NEAR - 1):
        theirs = (rank + s + 1) % NEAR
        copies.append(
            remote(
                grads.at[pl.ds(theirs * size, size)],
                near.at[s],
                sum_send.at[s],
                sum_recv.at[s],
                close[s],
            )
        )
    for copy in copies:
        copy.start()
    for copy in copies:
        copy.wait()
    summed = grads[pl.ds(rank * size, size), :]
    for s in range(NEAR - 1):
        summed = summed + near[s]
    part[...] = summed
    far[group] = summed
    copies = [
        remote(part, far.at[group], far_send.at[s], far_recv.at[s], distant[s])
        for s in range(FAR - 1)
    ]
    for copy in copies:
        copy.start()
    for copy in copies:
        copy.wait()
    summed = far[0]
    for s in range(1, FAR):
        summed = summed + far[s]
    mine = pl.ds(rank * size, size)
    whole[mine, :] = summed
    copies = [
        remote(whole.at[mine], whole.at[mine], all_send.at[s], all_recv.at[s], close[s])
        for s in range(NEAR - 1)
    ]
    for copy in copies:
        copy.start()
    for copy in copies:
        copy.wait()
    out_ref[...] = whole[...].reshape(4, H, H)


def grand_total(n, m0, u0, m1, u1, number):
    size = 4 * H // NEAR
    return pl.pallas_call(
        functools.partial(total_kernel, n),
        name="grand_total",
        out_shape=shape((4, H, H), F32),
        in_specs=[VMEM] * 4,
        out_specs=VMEM,
        scratch_shapes=[
            pltpu.VMEM((4 * H, H), F32),
            pltpu.VMEM((NEAR - 1, size, H), F32),
            pltpu.VMEM((size, H), F32),
            pltpu.VMEM((FAR, size, H), F32),
            pltpu.VMEM((4 * H, H), F32),
            DMA((NEAR - 1,)),
            DMA((NEAR - 1,)),
            DMA((FAR - 1,)),
            DMA((FAR - 1,)),
            DMA((NEAR - 1,)),
            DMA((NEAR - 1,)),
        ],
        compiler_params=params(8, collective_id=number, has_side_effects=True),
    )(m0, u0, m1, u1)


def per_device(
    n,
    features,
    cotangent,
    weights,
    fine_tiles,
    fine_columns,
    fine_halo,
    coarse_tiles,
    coarse_columns,
    coarse_halo,
    pair_send,
    members,
    coarse_count,
):
    fine_cols = fine_columns.reshape(-1)
    coarse_cols = coarse_columns.reshape(-1)
    h1, gate, slope, own, halo, z0, dz1 = forward(
        n,
        features,
        cotangent,
        weights,
        fine_cols,
        coarse_count,
        fine_halo,
        coarse_halo,
        pair_send,
        members,
        fine_tiles,
    )
    z1, dm1, piece1, update1 = coarse_level(own, halo, z0, dz1, weights, coarse_cols, coarse_tiles)
    arrived1 = send_back(n, piece1, 1)
    message1, lifted, away = coarse_back(
        dm1, arrived1, z0, dz1, z1, weights, coarse_count, coarse_halo, members
    )
    returned = send_back(n, away, 2)
    result, low, dm0, piece0, update0 = fine_level(
        lifted, returned, h1, cotangent, gate, slope, weights, fine_cols, pair_send, fine_tiles
    )
    arrived0 = send_back(n, piece0, 3)
    grad_features, message0 = fine_back(dm0, arrived0, features, low, weights, fine_halo)
    grads = grand_total(n, message0, update0, message1, update1, 4)
    return result, grad_features, grads


def solution(mesh):
    n = mesh.shape["dom"]
    placed = (
        P("dom", None),
        P("dom", None),
        P(),
        P("dom", None, None, None),
        P("dom", None, None),
        P("dom", None, None),
        P("dom", None, None, None),
        P("dom", None, None),
        P("dom", None, None),
        P("dom", None, None),
        P("dom", None, None),
        P("dom"),
    )
    return jax.shard_map(
        functools.partial(per_device, n),
        mesh=mesh,
        in_specs=placed,
        out_specs=(P("dom", None), P("dom", None), P()),
        check_vma=False,
    )
```

```python
import functools

import jax
import jax.numpy as jnp
from jax import lax
from jax.experimental import pallas as pl
from jax.experimental.pallas import tpu as pltpu
from jax.sharding import PartitionSpec as P

MESH = pl.DeviceIdType.MESH
OFFSETS = (1, -1, 8, -8)
F32, BF16, I32 = jnp.float32, jnp.bfloat16, jnp.int32
VMEM = pl.BlockSpec(memory_space=pltpu.VMEM)
SMEM = pl.BlockSpec(memory_space=pltpu.SMEM)
ANY = pl.BlockSpec(memory_space=pl.ANY)
DMA = pltpu.SemaphoreType.DMA
H = 128
T = 128
KT = 12
FB = 32
CB = 20
NF = FB * T
NC = CB * T
SEND = 256
HALO = 4 * SEND
QUAD = 4 * T
UNROLL = 16
NN = (((1,), (0,)), ((), ()))
NT = (((1,), (1,)), ((), ()))
TN = (((0,), (0,)), ((), ()))


def dot(a, b, how=NN):
    return lax.dot_general(a, b, how, preferred_element_type=F32)


def shape(dims, dtype):
    return jax.ShapeDtypeStruct(dims, dtype)


def params(mib=56, **more):
    return pltpu.CompilerParams(vmem_limit_bytes=mib * 2**20, **more)


def neighbour(me, n, offset):
    return lax.rem(me + (offset + n), n)


def greet(me, n):
    barrier = pltpu.get_barrier_semaphore()
    for offset in OFFSETS:
        pl.semaphore_signal(
            barrier, inc=1, device_id=(neighbour(me, n, offset),), device_id_type=MESH
        )
    return barrier


def remote(src, dst, send_sem, recv_sem, target):
    return pltpu.make_async_remote_copy(
        src_ref=src,
        dst_ref=dst,
        send_sem=send_sem,
        recv_sem=recv_sem,
        device_id=(target,),
        device_id_type=MESH,
    )


def index_copies(pairs, sem):
    copies = []
    for src, dst in pairs:
        width = src.shape[2]
        for j in range(src.shape[1]):
            copies.append((src.at[0, j], dst.at[pl.ds(j * width, width)]))
    return [pltpu.make_async_copy(a, b, sem.at[i]) for i, (a, b) in enumerate(copies)]


def loop(count, body, unroll=1):
    def step(i, carry):
        body(i)
        return carry

    lax.fori_loop(0, count, step, 0, unroll=unroll)


def gather_rows(index, first, source, target, count, step=1, shift=0):
    def body(i):
        base = pl.multiple_of(i * UNROLL, UNROLL)
        rows = [
            source[pl.ds(index[first + base + u] * step + shift, 1), :] for u in range(UNROLL)
        ]
        for u in range(UNROLL):
            target[pl.ds(base + u, 1), :] = rows[u]

    loop(count // UNROLL, body)


def block_row(tiles, columns, blocks, b):
    lhs = jnp.concatenate([tiles[b, k] for k in range(KT)], axis=1)
    rhs = jnp.concatenate([blocks[columns[k, 0, b]] for k in range(KT)], axis=0)
    return dot(lhs, rhs)


def spread_row(tiles, columns, grads_t, b, total):
    for k in range(KT):
        c = columns[k, 0, b]
        total[c] = total[c] + dot(grads_t, tiles[b, k])


def tile_copies(source, buffer, sem, count):
    size = source.shape[0] // count
    return [
        pltpu.make_async_copy(
            source.at[pl.ds(i * size, size)], buffer.at[pl.ds(i * size, size)], sem.at[i]
        )
        for i in range(count)
    ]


def wait_tiles(source, buffer, sem, i, size):
    pltpu.make_async_copy(
        source.at[pl.ds(i * size, size)], buffer.at[pl.ds(i * size, size)], sem.at[i]
    ).wait()


def forward_kernel(
    n,
    values,
    cot,
    weights,
    columns_hbm,
    count,
    fine_halo,
    coarse_halo,
    pair_send,
    members,
    tiles,
    h1_out,
    gate_out,
    slope_out,
    own_out,
    halo_out,
    z0_out,
    dz1_out,
    buf,
    ext,
    rows32,
    pairs,
    cells,
    stage,
    send_fine,
    send_cot,
    recv_cot,
    send_pair,
    recv_pair,
    send_coarse,
    recv_coarse,
    s_fine,
    s_coarse,
    s_pair,
    s_members,
    columns,
    tile_sem,
    index_sem,
    send_sem,
    recv_sem,
):
    me = lax.axis_index("dom")
    barrier = greet(me, n)
    index = index_copies(
        [(fine_halo, s_fine), (coarse_halo, s_coarse), (pair_send, s_pair), (members, s_members)],
        index_sem,
    )
    index.append(pltpu.make_async_copy(columns_hbm, columns, index_sem.at[14]))
    for copy in index:
        copy.start()
    for copy in tile_copies(tiles, buf, tile_sem, 8):
        copy.start()

    def project(i):
        at = pl.ds(i * QUAD, QUAD)
        low = dot(values[at, :], weights[0]).astype(BF16)
        rows32[at, :] = low.astype(F32)
        ext[pl.ds(i * 4, 4)] = low.reshape(4, T, H)

    loop(NF // QUAD, project)
    for copy in index:
        copy.wait()
    pl.semaphore_wait(barrier, 4)

    targets = [neighbour(me, n, offset) for offset in OFFSETS]
    fine = []
    for j in range(4):
        gather_rows(s_fine, j * SEND, rows32, stage, SEND)
        send_fine[pl.ds(2 * j, 2)] = stage[:SEND, :].astype(BF16).reshape(2, T, H)
        copy = remote(
            send_fine.at[pl.ds(2 * j, 2)],
            ext.at[pl.ds(FB + 2 * j, 2)],
            send_sem.at[j],
            recv_sem.at[j],
            targets[j],
        )
        copy.start()
        fine.append(copy)

    def place_cot(i):
        pairs[pl.ds(i * 2 * QUAD + 1, QUAD, stride=2), :] = cot[pl.ds(i * QUAD, QUAD), :].astype(F32)

    loop(NF // QUAD, place_cot)

    def exchange_pairs(shift, sent, received, first):
        copies = []
        for j in range(4):
            gather_rows(s_pair, j * SEND, pairs, stage, SEND, 2, shift)
            sent[j] = stage[:SEND, :].astype(BF16)
            copy = remote(
                sent.at[j],
                received.at[j],
                send_sem.at[first + j],
                recv_sem.at[first + j],
                targets[j],
            )
            copy.start()
            copies.append(copy)
        return copies

    paired_cot = exchange_pairs(1, send_cot, recv_cot, 12)
    for copy in fine:
        copy.wait()

    def level(i):
        wait_tiles(tiles, buf, tile_sem, i, 4)
        parts = []
        for q in range(4):
            b = i * 4 + q
            parts.append(block_row(buf, columns, ext, b))
        summed = jnp.concatenate(parts, axis=0)
        sigma = jax.nn.sigmoid(summed)
        gate = (summed * sigma).astype(BF16)
        at = pl.ds(i * QUAD, QUAD)
        gate_out[at, :] = gate
        slope_out[at, :] = (sigma * (1.0 + summed * (1.0 - sigma))).astype(BF16)
        out = (values[at, :].astype(F32) + dot(gate, weights[1])).astype(BF16)
        h1_out[at, :] = out
        pairs[pl.ds(i * 2 * QUAD, QUAD, stride=2), :] = out.astype(F32)

    loop(8, level)

    paired = exchange_pairs(0, send_pair, recv_pair, 4)
    for shift, copies, received in ((1, paired_cot, recv_cot), (0, paired, recv_pair)):
        for j in range(4):
            copies[j].wait()
            pairs[pl.ds(2 * (NF + j * SEND) + shift, SEND, stride=2), :] = received[j].astype(F32)

    def pool(i):
        base = pl.multiple_of(i * UNROLL, UNROLL)
        first = [pairs[pl.ds(s_members[base + u] * 2, 2), :] for u in range(UNROLL)]
        second = [pairs[pl.ds(s_members[NC + base + u] * 2, 2), :] for u in range(UNROLL)]
        for u in range(UNROLL):
            cells[pl.ds((base + u) * 2, 2), :] = first[u] + second[u]

    loop(NC // UNROLL, pool)
    live = count[0]

    def pooled(i):
        at = pl.ds(i * QUAD, QUAD)
        row = lax.broadcasted_iota(I32, (QUAD, H), 0) + i * QUAD
        alive = row < live
        z0 = jnp.where(alive, cells[pl.ds(i * 2 * QUAD, QUAD, stride=2), :], 0.0).astype(BF16)
        z0_out[at, :] = z0
        dz1_out[at, :] = jnp.where(
            alive, cells[pl.ds(i * 2 * QUAD + 1, QUAD, stride=2), :], 0.0
        ).astype(BF16)
        low = dot(z0, weights[2]).astype(BF16)
        rows32[at, :] = low.astype(F32)
        own_out[pl.ds(i * 4, 4)] = low.reshape(4, T, H)

    loop(NC // QUAD, pooled)
    coarse = []
    for j in range(4):
        gather_rows(s_coarse, j * SEND, rows32, stage, SEND)
        send_coarse[pl.ds(2 * j, 2)] = stage[:SEND, :].astype(BF16).reshape(2, T, H)
        copy = remote(
            send_coarse.at[pl.ds(2 * j, 2)],
            recv_coarse.at[pl.ds(2 * j, 2)],
            send_sem.at[8 + j],
            recv_sem.at[8 + j],
            targets[j],
        )
        copy.start()
        coarse.append(copy)
    for copy in coarse:
        copy.wait()
    halo_out[...] = recv_coarse[...]


def forward(n, values, cot, weights, columns, count, fine_halo, coarse_halo, pair_send, members, tiles):
    return pl.pallas_call(
        functools.partial(forward_kernel, n),
        name="forward",
        out_shape=[
            shape((NF, H), BF16),
            shape((NF, H), BF16),
            shape((NF, H), BF16),
            shape((CB, T, H), BF16),
            shape((8, T, H), BF16),
            shape((NC, H), BF16),
            shape((NC, H), BF16),
        ],
        in_specs=[VMEM, VMEM, VMEM, ANY, SMEM, ANY, ANY, ANY, ANY, ANY],
        out_specs=[VMEM] * 7,
        scratch_shapes=[
            pltpu.VMEM((FB, KT, T, T), BF16),
            pltpu.VMEM((FB + 8, T, H), BF16),
            pltpu.VMEM((NF, H), F32),
            pltpu.VMEM((2 * (NF + HALO), H), F32),
            pltpu.VMEM((2 * NC, H), F32),
            pltpu.VMEM((2 * SEND, H), F32),
            pltpu.VMEM((8, T, H), BF16),
            pltpu.VMEM((4, SEND, H), BF16),
            pltpu.VMEM((4, SEND, H), BF16),
            pltpu.VMEM((4, SEND, H), BF16),
            pltpu.VMEM((4, SEND, H), BF16),
            pltpu.VMEM((8, T, H), BF16),
            pltpu.VMEM((8, T, H), BF16),
            pltpu.SMEM((HALO,), I32),
            pltpu.SMEM((HALO,), I32),
            pltpu.SMEM((HALO,), I32),
            pltpu.SMEM((2 * NC,), I32),
            pltpu.SMEM((KT, 1, FB), I32),
            DMA((8,)),
            DMA((15,)),
            DMA((16,)),
            DMA((16,)),
        ],
        compiler_params=params(collective_id=0, has_side_effects=True),
    )(values, cot, weights, columns, count, fine_halo, coarse_halo, pair_send, members, tiles)


def rows_out(total, blocks, own_ref, halo_ref):
    def own(c):
        own_ref[pl.ds(c * T, T), :] = jnp.transpose(total[c])

    loop(blocks, own, 4)

    def halo(c):
        halo_ref[pl.ds(c * T, T), :] = jnp.transpose(total[blocks + c]).astype(BF16)

    loop(8, halo, 4)


def coarse_kernel(
    own,
    halo,
    z0,
    dz1,
    weights,
    columns_hbm,
    tiles,
    z1_out,
    dm_out,
    piece_out,
    update_out,
    buf,
    ext,
    gates,
    total,
    columns,
    tile_sem,
    index_sem,
):
    index = pltpu.make_async_copy(columns_hbm, columns, index_sem)
    index.start()
    for copy in tile_copies(tiles, buf, tile_sem, 5):
        copy.start()
    ext[pl.ds(0, CB)] = own[...]
    ext[pl.ds(CB, 8)] = halo[...]
    total[...] = jnp.zeros_like(total)
    index.wait()

    def level(i):
        wait_tiles(tiles, buf, tile_sem, i, 4)
        parts = []
        for q in range(4):
            b = i * 4 + q
            parts.append(block_row(buf, columns, ext, b))
        summed = jnp.concatenate(parts, axis=0)
        sigma = jax.nn.sigmoid(summed)
        gate = (summed * sigma).astype(BF16)
        at = pl.ds(i * QUAD, QUAD)
        gates[at, :] = gate
        z1_out[at, :] = (z0[at, :].astype(F32) + dot(gate, weights[3])).astype(BF16)
        slope = sigma * (1.0 + summed * (1.0 - sigma))
        grads = (dot(dz1[at, :], weights[3], NT) * slope).astype(BF16)
        for q in range(4):
            b = i * 4 + q
            grads_t = jnp.transpose(grads[q * T : (q + 1) * T, :])
            spread_row(buf, columns, grads_t, b, total)

    loop(CB // 4, level)
    rows_out(total, CB, dm_out, piece_out)
    update_out[...] = dot(gates[...], dz1[...], TN)


def coarse_level(own, halo, z0, dz1, weights, columns, tiles):
    return pl.pallas_call(
        coarse_kernel,
        name="coarse_level",
        out_shape=[
            shape((NC, H), BF16),
            shape((NC, H), F32),
            shape((HALO, H), BF16),
            shape((H, H), F32),
        ],
        in_specs=[VMEM, VMEM, VMEM, VMEM, VMEM, ANY, ANY],
        out_specs=[VMEM] * 4,
        scratch_shapes=[
            pltpu.VMEM((CB, KT, T, T), BF16),
            pltpu.VMEM((CB + 8, T, H), BF16),
            pltpu.VMEM((NC, H), BF16),
            pltpu.VMEM((CB + 8, T, H), F32),
            pltpu.SMEM((KT, 1, CB), I32),
            DMA((5,)),
            DMA,
        ],
        compiler_params=params(),
    )(own, halo, z0, dz1, weights, columns, tiles)


def loads(pairs, sem):
    return [pltpu.make_async_copy(src, dst, sem.at[i]) for i, (src, dst) in enumerate(pairs)]


def lane_row(index):
    return jnp.concatenate([index[0, j : j + 1, :] for j in range(4)], axis=1)


def returned_rows(named, arrived, base, count):
    row = lax.broadcasted_iota(I32, (count, HALO), 0)
    chosen = jnp.where(jnp.broadcast_to(named - base, (count, HALO)) == row, 1.0, 0.0).astype(BF16)
    return dot(chosen, arrived)


WIDE = 512
ROWS = 48


def placed(rows, numbers):
    high, low = rows // T, rows % T
    at = jnp.broadcast_to(high, (ROWS, WIDE)) == lax.broadcasted_iota(I32, (ROWS, WIDE), 0)
    parts = [
        jnp.where(at, jnp.broadcast_to(part.astype(F32), (ROWS, WIDE)), 0.0).astype(BF16)
        for part in (numbers // 64, numbers % 64)
    ]
    lanes = jnp.where(
        jnp.broadcast_to(low, (T, WIDE)) == lax.broadcasted_iota(I32, (T, WIDE), 0), 1.0, 0.0
    ).astype(BF16)
    return dot(jnp.concatenate(parts, axis=0), lanes, NT)


def whole(tables):
    return (tables[:ROWS] * 64.0 + tables[ROWS:]).astype(I32)


def sources(members, pair_send, live):
    nowhere = ROWS * T - 1
    cells = jnp.zeros((2 * ROWS, T), F32)
    for j in range(2):
        for k in range(NC // WIDE):
            cell = lax.broadcasted_iota(I32, (1, WIDE), 1) + k * WIDE
            row = members[0, j : j + 1, k * WIDE : (k + 1) * WIDE]
            cells = cells + placed(jnp.where(cell < live, row, nowhere), cell + 1)
    slots = jnp.zeros((2 * ROWS, T), F32)
    sent = lane_row(pair_send)
    for k in range(HALO // WIDE):
        slot = lax.broadcasted_iota(I32, (1, WIDE), 1) + (NC + k * WIDE)
        slots = slots + placed(sent[:, k * WIDE : (k + 1) * WIDE], slot + 1)
    cells, slots = whole(cells), whole(slots)
    found = jnp.where(cells > 0, cells, jnp.where(slots > 0, slots, NC + HALO + 1)) - 1
    return jnp.minimum(found, NC + HALO)


def gather_block(index, block, source, target, first, width=2, shift=0):
    for g in range(T // UNROLL):
        rows = [
            source[pl.ds(index[block, g * UNROLL + u] * 2 + shift, width), :]
            for u in range(UNROLL)
        ]
        for u in range(UNROLL):
            target[pl.ds((first + g * UNROLL + u) * width, width), :] = rows[u]


def coarse_back_kernel(
    n,
    weights,
    count,
    coarse_halo,
    pair_send,
    members,
    pieces,
    dm,
    z0_hbm,
    dz1_hbm,
    z1_hbm,
    h1_hbm,
    cot_hbm,
    gate_hbm,
    slope_hbm,
    result_out,
    low_out,
    grads_out,
    message_out,
    update_out,
    arrived,
    rows,
    z0,
    dz1,
    z1,
    h1,
    cot,
    gate,
    slope,
    cells,
    stage,
    send_out,
    recv_out,
    send_away,
    recv_away,
    table,
    source,
    load_sem,
    index_sem,
    send_sem,
    recv_sem,
):
    me = lax.axis_index("dom")
    barrier = greet(me, n)
    early = loads([(dm, rows), (z0_hbm, z0), (dz1_hbm, dz1), (z1_hbm, z1)], load_sem)
    later = loads(
        [(h1_hbm, h1), (cot_hbm, cot), (gate_hbm, gate), (slope_hbm, slope)],
        load_sem.at[pl.ds(4, 4)],
    )
    for copy in early + later:
        copy.start()
    targets = [neighbour(me, n, -offset) for offset in OFFSETS]
    pl.semaphore_wait(barrier, 4)
    back = [
        remote(
            pieces.at[pl.ds(j * SEND, SEND)],
            arrived.at[pl.ds(j * SEND, SEND)],
            send_sem.at[j],
            recv_sem.at[j],
            targets[j],
        )
        for j in range(4)
    ]
    for copy in back:
        copy.start()
    table[...] = sources(members, pair_send, count[0])
    index = pltpu.make_async_copy(table, source, index_sem)
    index.start()
    cells[pl.ds(2 * (NC + HALO), 16), :] = jnp.zeros((16, H), F32)
    message_out[...] = jnp.zeros_like(message_out)
    update_out[...] = jnp.zeros_like(update_out)
    named = lane_row(coarse_halo)
    for copy in early:
        copy.wait()

    def place(i):
        cells[pl.ds(i * 2 * QUAD, QUAD, stride=2), :] = z1[pl.ds(i * QUAD, QUAD), :].astype(F32)

    loop(NC // QUAD, place)

    def exchange_away(shift, sent, received, first):
        copies = []
        for j in range(4):
            loop(
                2,
                lambda t: gather_block(source, FB + 2 * j + t, cells, stage, t * T, 1, shift),
            )
            sent[j] = stage[:SEND, :].astype(BF16)
            copy = remote(
                sent.at[j],
                received.at[j],
                send_sem.at[first + j],
                recv_sem.at[first + j],
                targets[j],
            )
            copy.start()
            copies.append(copy)
        return copies

    index.wait()
    away_out = exchange_away(0, send_out, recv_out, 8)
    for copy in back:
        copy.wait()

    def retract(i):
        at = pl.ds(i * QUAD, QUAD)
        parts = [
            rows[pl.ds(i * QUAD + q * SEND, SEND), :]
            + returned_rows(named, arrived[...], i * QUAD + q * SEND, SEND)
            for q in range(2)
        ]
        low = jnp.concatenate(parts, axis=0).astype(BF16)
        message_out[...] += dot(z0[at, :], low, TN)
        cells[pl.ds(i * 2 * QUAD + 1, QUAD, stride=2), :] = dz1[at, :].astype(F32) + dot(
            low, weights[2], NT
        )

    loop(NC // QUAD, retract)
    away = exchange_away(1, send_away, recv_away, 4)
    for copy in later:
        copy.wait()
    for shift, copies, received in ((0, away_out, recv_out), (1, away, recv_away)):
        for j in range(4):
            copies[j].wait()
            cells[pl.ds(2 * (NC + j * SEND) + shift, SEND, stride=2), :] = received[j].astype(F32)

    def lift(i):
        loop(4, lambda q: gather_block(source, i * 4 + q, cells, stage, q * T))
        at = pl.ds(i * QUAD, QUAD)
        result_out[at, :] = (
            h1[at, :].astype(F32) + stage[pl.ds(0, QUAD, stride=2), :]
        ).astype(BF16)
        low = (cot[at, :].astype(F32) + stage[pl.ds(1, QUAD, stride=2), :]).astype(BF16)
        low_out[at, :] = low
        update_out[...] += dot(gate[at, :], low, TN)
        grads_out[at, :] = (dot(low, weights[1], NT) * slope[at, :].astype(F32)).astype(BF16)

    loop(NF // QUAD, lift)


def coarse_back(
    n, number, weights, count, coarse_halo, pair_send, members, pieces, dm, z0, dz1, z1, h1, cot, gate, slope
):
    return pl.pallas_call(
        functools.partial(coarse_back_kernel, n),
        name="coarse_back",
        out_shape=[
            shape((NF, H), BF16),
            shape((NF, H), BF16),
            shape((NF, H), BF16),
            shape((H, H), F32),
            shape((H, H), F32),
        ],
        in_specs=[VMEM, SMEM, VMEM, VMEM, VMEM] + [ANY] * 9,
        out_specs=[VMEM] * 5,
        scratch_shapes=[
            pltpu.VMEM((HALO, H), BF16),
            pltpu.VMEM((NC, H), F32),
            pltpu.VMEM((NC, H), BF16),
            pltpu.VMEM((NC, H), BF16),
            pltpu.VMEM((NC, H), BF16),
            pltpu.VMEM((NF, H), BF16),
            pltpu.VMEM((NF, H), BF16),
            pltpu.VMEM((NF, H), BF16),
            pltpu.VMEM((NF, H), BF16),
            pltpu.VMEM((2 * (NC + HALO) + 16, H), F32),
            pltpu.VMEM((2 * QUAD, H), F32),
            pltpu.VMEM((4, SEND, H), BF16),
            pltpu.VMEM((4, SEND, H), BF16),
            pltpu.VMEM((4, SEND, H), BF16),
            pltpu.VMEM((4, SEND, H), BF16),
            pltpu.VMEM((ROWS, T), I32),
            pltpu.SMEM((ROWS, T), I32),
            DMA((8,)),
            DMA,
            DMA((12,)),
            DMA((12,)),
        ],
        compiler_params=params(collective_id=number, has_side_effects=True),
    )(weights, count, coarse_halo, pair_send, members, pieces, dm, z0, dz1, z1, h1, cot, gate, slope)


def fine_kernel(
    grads,
    columns_hbm,
    tiles,
    result,
    dm_out,
    piece_out,
    result_out,
    buf,
    total,
    held,
    columns,
    index_sem,
    result_sem,
    tile_sem,
):
    index = pltpu.make_async_copy(columns_hbm, columns, index_sem)
    index.start()
    for copy in tile_copies(tiles, buf, tile_sem, 8):
        copy.start()
    taken = pltpu.make_async_copy(result, held, result_sem.at[0])
    taken.start()
    total[...] = jnp.zeros_like(total)
    index.wait()

    def level(i):
        wait_tiles(tiles, buf, tile_sem, i, 4)
        for q in range(4):
            b = i * 4 + q
            spread_row(buf, columns, jnp.transpose(grads[pl.ds(b * T, T), :]), b, total)

    loop(4, level)
    taken.wait()
    passed = pltpu.make_async_copy(held, result_out, result_sem.at[1])
    passed.start()
    loop(4, lambda i: level(i + 4))
    rows_out(total, FB, dm_out, piece_out)
    passed.wait()


def fine_spread(grads, columns, tiles, result):
    return pl.pallas_call(
        fine_kernel,
        name="fine_spread",
        out_shape=[shape((NF, H), F32), shape((HALO, H), BF16), shape((NF, H), BF16)],
        in_specs=[VMEM, ANY, ANY, ANY],
        out_specs=[VMEM, VMEM, ANY],
        scratch_shapes=[
            pltpu.VMEM((FB, KT, T, T), BF16),
            pltpu.VMEM((FB + 8, T, H), F32),
            pltpu.VMEM((NF, H), BF16),
            pltpu.SMEM((KT, 1, FB), I32),
            DMA,
            DMA((2,)),
            DMA((8,)),
        ],
        compiler_params=params(),
    )(grads, columns, tiles, result)


NEAR = 8
FAR = 16


def scatter_near(grads, near, send, recv, rank, close):
    size = near.shape[1]
    copies = [
        remote(
            grads.at[pl.ds((rank + s + 1) % NEAR * size, size)],
            near.at[s],
            send.at[s],
            recv.at[s],
            close[s],
        )
        for s in range(NEAR - 1)
    ]
    for copy in copies:
        copy.start()
    return copies


def share_far(copies, grads, near, part, far, send, recv, rank, group, distant):
    for copy in copies:
        copy.wait()
    size = near.shape[1]
    summed = grads[pl.ds(rank * size, size), :]
    for s in range(NEAR - 1):
        summed = summed + near[s]
    part[...] = summed
    far[group] = summed
    copies = [
        remote(part, far.at[group], send.at[s], recv.at[s], distant[s]) for s in range(FAR - 1)
    ]
    for copy in copies:
        copy.start()
    return copies


def gather_near(copies, far, total, send, recv, rank, close):
    for copy in copies:
        copy.wait()
    size = far.shape[1]
    summed = far[0]
    for s in range(1, FAR):
        summed = summed + far[s]
    mine = pl.ds(rank * size, size)
    total[mine, :] = summed
    copies = [
        remote(total.at[mine], total.at[mine], send.at[s], recv.at[s], close[s])
        for s in range(NEAR - 1)
    ]
    for copy in copies:
        copy.start()
    return copies


def fine_back_kernel(
    n,
    weights,
    fine_halo,
    u0,
    m1,
    u1,
    pieces,
    dm,
    values_hbm,
    low_hbm,
    grad_out,
    total_out,
    arrived,
    rows,
    values,
    low,
    messages,
    first,
    first_near,
    first_part,
    first_far,
    first_total,
    last,
    last_near,
    last_part,
    last_far,
    last_total,
    load_sem,
    send_sem,
    recv_sem,
    near_send,
    near_recv,
    far_send,
    far_recv,
    all_send,
    all_recv,
):
    me = lax.axis_index("dom")
    group, rank = me // NEAR, me % NEAR
    close = [group * NEAR + (rank + s) % NEAR for s in range(1, NEAR)]
    distant = [((group + s) % FAR) * NEAR + rank for s in range(1, FAR)]
    barrier = greet(me, n)
    for target in close + distant:
        pl.semaphore_signal(barrier, inc=1, device_id=(target,), device_id_type=MESH)
    copies = loads([(dm, rows), (values_hbm, values), (low_hbm, low)], load_sem)
    for copy in copies:
        copy.start()
    for i, ref in enumerate((u0, m1, u1)):
        first[pl.ds(i * H, H), :] = ref[...]
    last[...] = jnp.zeros_like(last)
    named = lane_row(fine_halo)
    pl.semaphore_wait(barrier, 4 + NEAR - 1 + FAR - 1)
    back = [
        remote(
            pieces.at[pl.ds(j * SEND, SEND)],
            arrived.at[pl.ds(j * SEND, SEND)],
            send_sem.at[j],
            recv_sem.at[j],
            neighbour(me, n, -OFFSETS[j]),
        )
        for j in range(4)
    ]
    for copy in back:
        copy.start()
    near1 = scatter_near(first, first_near, near_send.at[0], near_recv.at[0], rank, close)
    for copy in copies + back:
        copy.wait()

    def retract(i):
        at = pl.ds(i * QUAD, QUAD)
        parts = [
            rows[pl.ds(i * QUAD + q * SEND, SEND), :]
            + returned_rows(named, arrived[...], i * QUAD + q * SEND, SEND)
            for q in range(2)
        ]
        part = jnp.concatenate(parts, axis=0).astype(BF16)
        last[...] += dot(values[at, :], part, TN)
        messages[at, :] = part

    def grads(i):
        at = pl.ds(i * QUAD, QUAD)
        grad_out[at, :] = (low[at, :].astype(F32) + dot(messages[at, :], weights[0], NT)).astype(BF16)

    loop(4, retract)
    far1 = share_far(
        near1, first, first_near, first_part, first_far, far_send.at[0], far_recv.at[0], rank, group, distant
    )
    loop(4, lambda i: retract(i + 4))
    near2 = scatter_near(last, last_near, near_send.at[1], near_recv.at[1], rank, close)
    loop(4, grads)
    all1 = gather_near(far1, first_far, first_total, all_send.at[0], all_recv.at[0], rank, close)
    far2 = share_far(
        near2, last, last_near, last_part, last_far, far_send.at[1], far_recv.at[1], rank, group, distant
    )
    loop(4, lambda i: grads(i + 4))
    all2 = gather_near(far2, last_far, last_total, all_send.at[1], all_recv.at[1], rank, close)
    for copy in all1:
        copy.wait()
    total_out[pl.ds(1, 3)] = first_total[...].reshape(3, H, H)
    for copy in all2:
        copy.wait()
    total_out[0] = last_total[...]


def fine_back(n, number, weights, fine_halo, u0, m1, u1, pieces, dm, values, low):
    one, two = 3 * H // NEAR, H // NEAR
    sums = []
    for count, size in ((3 * H, one), (H, two)):
        sums += [
            pltpu.VMEM((count, H), F32),
            pltpu.VMEM((NEAR - 1, size, H), F32),
            pltpu.VMEM((size, H), F32),
            pltpu.VMEM((FAR, size, H), F32),
            pltpu.VMEM((count, H), F32),
        ]
    return pl.pallas_call(
        functools.partial(fine_back_kernel, n),
        name="fine_back",
        out_shape=[shape((NF, H), BF16), shape((4, H, H), F32)],
        in_specs=[VMEM] * 5 + [ANY] * 4,
        out_specs=[VMEM] * 2,
        scratch_shapes=[
            pltpu.VMEM((HALO, H), BF16),
            pltpu.VMEM((NF, H), F32),
            pltpu.VMEM((NF, H), BF16),
            pltpu.VMEM((NF, H), BF16),
            pltpu.VMEM((NF, H), BF16),
        ]
        + sums
        + [
            DMA((3,)),
            DMA((4,)),
            DMA((4,)),
            DMA((2, NEAR - 1)),
            DMA((2, NEAR - 1)),
            DMA((2, FAR - 1)),
            DMA((2, FAR - 1)),
            DMA((2, NEAR - 1)),
            DMA((2, NEAR - 1)),
        ],
        compiler_params=params(collective_id=number, has_side_effects=True),
    )(weights, fine_halo, u0, m1, u1, pieces, dm, values, low)


def finish_kernel(grad, totals, grad_out, totals_out):
    grad_out[...] = grad[...]
    totals_out[...] = totals[...]


def finish(grad, totals):
    return pl.pallas_call(
        finish_kernel,
        name="finish",
        out_shape=[shape(grad.shape, grad.dtype), shape(totals.shape, totals.dtype)],
        in_specs=[VMEM] * 2,
        out_specs=[VMEM] * 2,
        compiler_params=params(),
    )(grad, totals)


def per_device(
    n,
    features,
    cotangent,
    weights,
    fine_tiles,
    fine_columns,
    fine_halo,
    coarse_tiles,
    coarse_columns,
    coarse_halo,
    pair_send,
    members,
    coarse_count,
):
    fine_cols = jnp.transpose(fine_columns, (2, 0, 1))
    coarse_cols = jnp.transpose(coarse_columns, (2, 0, 1))
    h1, gate, slope, own, halo, z0, dz1 = forward(
        n,
        features,
        cotangent,
        weights,
        fine_cols,
        coarse_count,
        fine_halo,
        coarse_halo,
        pair_send,
        members,
        fine_tiles,
    )
    z1, dm1, piece1, update1 = coarse_level(own, halo, z0, dz1, weights, coarse_cols, coarse_tiles)
    result, low, grads, message1, update0 = coarse_back(
        n,
        1,
        weights,
        coarse_count,
        coarse_halo,
        pair_send,
        members,
        piece1,
        dm1,
        z0,
        dz1,
        z1,
        h1,
        cotangent,
        gate,
        slope,
    )
    dm0, piece0, result = fine_spread(grads, fine_cols, fine_tiles, result)
    grad_features, totals = fine_back(
        n, 2, weights, fine_halo, update0, message1, update1, piece0, dm0, features, low
    )
    grad_features, totals = finish(grad_features, totals)
    return result, grad_features, totals


def solution(mesh):
    n = mesh.shape["dom"]
    placed = (
        P("dom", None),
        P("dom", None),
        P(),
        P("dom", None, None, None),
        P("dom", None, None),
        P("dom", None, None),
        P("dom", None, None, None),
        P("dom", None, None),
        P("dom", None, None),
        P("dom", None, None),
        P("dom", None, None),
        P("dom"),
    )
    return jax.shard_map(
        functools.partial(per_device, n),
        mesh=mesh,
        in_specs=placed,
        out_specs=(P("dom", None), P("dom", None), P()),
        check_vma=False,
    )
```

```python
import functools

import jax
import jax.numpy as jnp
from jax import lax
from jax.experimental import pallas as pl
from jax.experimental.pallas import tpu as pltpu
from jax.sharding import PartitionSpec as P

MESH = pl.DeviceIdType.MESH
OFFSETS = (1, -1, 8, -8)
F32, BF16, I32 = jnp.float32, jnp.bfloat16, jnp.int32
VMEM = pl.BlockSpec(memory_space=pltpu.VMEM)
SMEM = pl.BlockSpec(memory_space=pltpu.SMEM)
ANY = pl.BlockSpec(memory_space=pl.ANY)
DMA = pltpu.SemaphoreType.DMA
H = 128
T = 128
KT = 12
FB = 32
CB = 20
NF = FB * T
NC = CB * T
SEND = 256
HALO = 4 * SEND
QUAD = 4 * T
UNROLL = 16
NN = (((1,), (0,)), ((), ()))
NT = (((1,), (1,)), ((), ()))
TN = (((0,), (0,)), ((), ()))


def dot(a, b, how=NN):
    return lax.dot_general(a, b, how, preferred_element_type=F32)


def shape(dims, dtype):
    return jax.ShapeDtypeStruct(dims, dtype)


def params(mib=56, **more):
    return pltpu.CompilerParams(vmem_limit_bytes=mib * 2**20, **more)


def neighbour(me, n, offset):
    return lax.rem(me + (offset + n), n)


def greet(me, n):
    barrier = pltpu.get_barrier_semaphore()
    for offset in OFFSETS:
        pl.semaphore_signal(
            barrier, inc=1, device_id=(neighbour(me, n, offset),), device_id_type=MESH
        )
    return barrier


def remote(src, dst, send_sem, recv_sem, target):
    return pltpu.make_async_remote_copy(
        src_ref=src,
        dst_ref=dst,
        send_sem=send_sem,
        recv_sem=recv_sem,
        device_id=(target,),
        device_id_type=MESH,
    )


def index_copies(pairs, sem):
    copies = []
    for src, dst in pairs:
        width = src.shape[2]
        for j in range(src.shape[1]):
            copies.append((src.at[0, j], dst.at[pl.ds(j * width, width)]))
    return [pltpu.make_async_copy(a, b, sem.at[i]) for i, (a, b) in enumerate(copies)]


def loop(count, body, unroll=1):
    def step(i, carry):
        body(i)
        return carry

    lax.fori_loop(0, count, step, 0, unroll=unroll)


def gather_rows(index, first, source, target, count, step=1, shift=0):
    def body(i):
        base = pl.multiple_of(i * UNROLL, UNROLL)
        rows = [
            source[pl.ds(index[first + base + u] * step + shift, 1), :] for u in range(UNROLL)
        ]
        for u in range(UNROLL):
            target[pl.ds(base + u, 1), :] = rows[u]

    loop(count // UNROLL, body)


def block_row(tiles, columns, blocks, b):
    lhs = jnp.concatenate([tiles[b, k] for k in range(KT)], axis=1)
    rhs = jnp.concatenate([blocks[columns[k, 0, b]] for k in range(KT)], axis=0)
    return dot(lhs, rhs)


def spread_row(tiles, columns, grads_t, b, total):
    for k in range(KT):
        c = columns[k, 0, b]
        total[c] = total[c] + dot(grads_t, tiles[b, k])


def tile_copies(source, buffer, sem, count):
    size = source.shape[0] // count
    return [
        pltpu.make_async_copy(
            source.at[pl.ds(i * size, size)], buffer.at[pl.ds(i * size, size)], sem.at[i]
        )
        for i in range(count)
    ]


def wait_tiles(source, buffer, sem, i, size):
    pltpu.make_async_copy(
        source.at[pl.ds(i * size, size)], buffer.at[pl.ds(i * size, size)], sem.at[i]
    ).wait()


def loads(pairs, sem):
    return [pltpu.make_async_copy(src, dst, sem.at[i]) for i, (src, dst) in enumerate(pairs)]


def forward_kernel(
    n,
    weights,
    count,
    values_hbm,
    cot_hbm,
    columns_hbm,
    fine_halo,
    coarse_halo,
    pair_send,
    members,
    tiles,
    h1_hbm,
    gate_hbm,
    slope_hbm,
    halo_out,
    z0_out,
    z0_halo_out,
    dz1_out,
    values,
    cot,
    h1,
    gates,
    slopes,
    buf,
    ext,
    rows32,
    pairs,
    cells,
    stage,
    send_fine,
    recv_fine,
    send_cot,
    recv_cot,
    send_pair,
    recv_pair,
    send_coarse,
    recv_coarse,
    s_fine,
    s_coarse,
    s_pair,
    s_members,
    columns,
    load_sem,
    store_sem,
    tile_sem,
    index_sem,
    send_sem,
    recv_sem,
):
    me = lax.axis_index("dom")
    barrier = greet(me, n)
    taken = loads([(values_hbm, values), (cot_hbm, cot)], load_sem)
    index = index_copies(
        [(fine_halo, s_fine), (coarse_halo, s_coarse), (pair_send, s_pair), (members, s_members)],
        index_sem,
    )
    index.append(pltpu.make_async_copy(columns_hbm, columns, index_sem.at[14]))
    for copy in taken[:1] + index + taken[1:]:
        copy.start()
    for copy in tile_copies(tiles, buf, tile_sem, 8):
        copy.start()
    taken[0].wait()

    def widen(i):
        at = pl.ds(i * QUAD, QUAD)
        rows32[at, :] = values[at, :].astype(F32)

    loop(NF // QUAD, widen)
    for copy in index:
        copy.wait()
    targets = [neighbour(me, n, offset) for offset in OFFSETS]

    def exchange(index, source, sent, received, first, step=1, shift=0, ready=None):
        copies = []
        for j in range(4):
            gather_rows(index, j * SEND, source, stage, SEND, step, shift)
            sent[j] = stage[...].astype(BF16)
            if ready is not None and j == 0:
                pl.semaphore_wait(ready, 4)
            copy = remote(
                sent.at[j],
                received.at[j],
                send_sem.at[first + j],
                recv_sem.at[first + j],
                targets[j],
            )
            copy.start()
            copies.append(copy)
        return copies

    fine = exchange(s_fine, rows32, send_fine, recv_fine, 0, ready=barrier)

    def project(i):
        at = pl.ds(i * QUAD, QUAD)
        ext[pl.ds(i * 4, 4)] = dot(values[at, :], weights[0]).astype(BF16).reshape(4, T, H)

    loop(NF // QUAD, project)
    taken[1].wait()

    def place_cot(i):
        pairs[pl.ds(i * 2 * QUAD + 1, QUAD, stride=2), :] = cot[pl.ds(i * QUAD, QUAD), :].astype(F32)

    loop(NF // QUAD, place_cot)
    paired_cot = exchange(s_pair, pairs, send_cot, recv_cot, 12, 2, 1)
    for j in range(4):
        fine[j].wait()
        ext[pl.ds(FB + 2 * j, 2)] = dot(recv_fine[j], weights[0]).astype(BF16).reshape(2, T, H)

    def level(i):
        wait_tiles(tiles, buf, tile_sem, i, 4)
        parts = []
        for q in range(4):
            b = i * 4 + q
            parts.append(block_row(buf, columns, ext, b))
        summed = jnp.concatenate(parts, axis=0)
        sigma = jax.nn.sigmoid(summed)
        gate = (summed * sigma).astype(BF16)
        at = pl.ds(i * QUAD, QUAD)
        gates[at, :] = gate
        slopes[at, :] = (sigma * (1.0 + summed * (1.0 - sigma))).astype(BF16)
        out = (values[at, :].astype(F32) + dot(gate, weights[1])).astype(BF16)
        h1[at, :] = out
        pairs[pl.ds(i * 2 * QUAD, QUAD, stride=2), :] = out.astype(F32)

    loop(8, level)
    paired = exchange(s_pair, pairs, send_pair, recv_pair, 4, 2, 0)
    stored = loads([(h1, h1_hbm), (gates, gate_hbm), (slopes, slope_hbm)], store_sem)
    for copy in stored:
        copy.start()
    halo_out[...] = recv_fine[...].reshape(HALO, H)
    for shift, copies, received in ((1, paired_cot, recv_cot), (0, paired, recv_pair)):
        for j in range(4):
            copies[j].wait()
            pairs[pl.ds(2 * (NF + j * SEND) + shift, SEND, stride=2), :] = received[j].astype(F32)

    def pool(i):
        base = pl.multiple_of(i * UNROLL, UNROLL)
        first = [pairs[pl.ds(s_members[base + u] * 2, 2), :] for u in range(UNROLL)]
        second = [pairs[pl.ds(s_members[NC + base + u] * 2, 2), :] for u in range(UNROLL)]
        for u in range(UNROLL):
            cells[pl.ds((base + u) * 2, 2), :] = first[u] + second[u]

    loop(NC // UNROLL, pool)
    live = count[0]

    def pooled(i):
        at = pl.ds(i * QUAD, QUAD)
        row = lax.broadcasted_iota(I32, (QUAD, H), 0) + i * QUAD
        z0 = jnp.where(row < live, cells[pl.ds(i * 2 * QUAD, QUAD, stride=2), :], 0.0).astype(BF16)
        z0_out[at, :] = z0
        rows32[at, :] = z0.astype(F32)

    loop(NC // QUAD, pooled)
    coarse = exchange(s_coarse, rows32, send_coarse, recv_coarse, 8)

    def pooled_cot(i):
        at = pl.ds(i * QUAD, QUAD)
        row = lax.broadcasted_iota(I32, (QUAD, H), 0) + i * QUAD
        dz1_out[at, :] = jnp.where(
            row < live, cells[pl.ds(i * 2 * QUAD + 1, QUAD, stride=2), :], 0.0
        ).astype(BF16)

    loop(NC // QUAD, pooled_cot)
    for copy in stored + coarse:
        copy.wait()
    z0_halo_out[...] = recv_coarse[...].reshape(HALO, H)


def forward(n, weights, count, values, cot, columns, fine_halo, coarse_halo, pair_send, members, tiles):
    return pl.pallas_call(
        functools.partial(forward_kernel, n),
        name="forward",
        out_shape=[
            shape((NF, H), BF16),
            shape((NF, H), BF16),
            shape((NF, H), BF16),
            shape((HALO, H), BF16),
            shape((NC, H), BF16),
            shape((HALO, H), BF16),
            shape((NC, H), BF16),
        ],
        in_specs=[VMEM, SMEM] + [ANY] * 8,
        out_specs=[ANY] * 3 + [VMEM] * 4,
        scratch_shapes=[pltpu.VMEM((NF, H), BF16)] * 5
        + [
            pltpu.VMEM((FB, KT, T, T), BF16),
            pltpu.VMEM((FB + 8, T, H), BF16),
            pltpu.VMEM((NF, H), F32),
            pltpu.VMEM((2 * (NF + HALO), H), F32),
            pltpu.VMEM((2 * NC, H), F32),
            pltpu.VMEM((SEND, H), F32),
        ]
        + [pltpu.VMEM((4, SEND, H), BF16)] * 8
        + [
            pltpu.SMEM((HALO,), I32),
            pltpu.SMEM((HALO,), I32),
            pltpu.SMEM((HALO,), I32),
            pltpu.SMEM((2 * NC,), I32),
            pltpu.SMEM((KT, 1, FB), I32),
            DMA((2,)),
            DMA((3,)),
            DMA((8,)),
            DMA((15,)),
            DMA((16,)),
            DMA((16,)),
        ],
        compiler_params=params(collective_id=0, has_side_effects=True),
    )(weights, count, values, cot, columns, fine_halo, coarse_halo, pair_send, members, tiles)


def rows_out(total, blocks, own_values, halo_values, own_ref, halo_ref, message_ref):
    def own(c):
        part = total[c]
        at = pl.ds(c * T, T)
        own_ref[at, :] = jnp.transpose(part)
        message_ref[...] += dot(part.astype(BF16), own_values[at, :])

    def halo(c):
        part = total[blocks + c]
        at = pl.ds(c * T, T)
        halo_ref[at, :] = jnp.transpose(part).astype(BF16)
        message_ref[...] += dot(part.astype(BF16), halo_values[at, :])

    message_ref[...] = jnp.zeros_like(message_ref)
    loop(blocks, own, 4)
    loop(8, halo, 4)
    message_ref[...] = jnp.transpose(message_ref[...])


def coarse_kernel(
    z0,
    z0_halo,
    dz1,
    weights,
    columns_hbm,
    tiles,
    z1_out,
    dm_out,
    piece_out,
    message_out,
    update_out,
    buf,
    ext,
    gates,
    total,
    columns,
    tile_sem,
    index_sem,
):
    index = pltpu.make_async_copy(columns_hbm, columns, index_sem)
    index.start()
    for copy in tile_copies(tiles, buf, tile_sem, 5):
        copy.start()

    def project(i):
        part = z0[pl.ds(i * QUAD, QUAD), :]
        ext[pl.ds(i * 4, 4)] = dot(part, weights[2]).astype(BF16).reshape(4, T, H)

    loop(CB // 4, project)
    ext[pl.ds(CB, 8)] = dot(z0_halo[...], weights[2]).astype(BF16).reshape(8, T, H)
    total[...] = jnp.zeros_like(total)
    index.wait()

    def level(i):
        wait_tiles(tiles, buf, tile_sem, i, 4)
        parts = []
        for q in range(4):
            b = i * 4 + q
            parts.append(block_row(buf, columns, ext, b))
        summed = jnp.concatenate(parts, axis=0)
        sigma = jax.nn.sigmoid(summed)
        gate = (summed * sigma).astype(BF16)
        at = pl.ds(i * QUAD, QUAD)
        gates[at, :] = gate
        z1_out[at, :] = (z0[at, :].astype(F32) + dot(gate, weights[3])).astype(BF16)
        slope = sigma * (1.0 + summed * (1.0 - sigma))
        grads = (dot(dz1[at, :], weights[3], NT) * slope).astype(BF16)
        for q in range(4):
            b = i * 4 + q
            grads_t = jnp.transpose(grads[q * T : (q + 1) * T, :])
            spread_row(buf, columns, grads_t, b, total)

    loop(CB // 4, level)
    rows_out(total, CB, z0, z0_halo, dm_out, piece_out, message_out)
    update_out[...] = dot(gates[...], dz1[...], TN)


def coarse_level(z0, z0_halo, dz1, weights, columns, tiles):
    return pl.pallas_call(
        coarse_kernel,
        name="coarse_level",
        out_shape=[
            shape((NC, H), BF16),
            shape((NC, H), F32),
            shape((HALO, H), BF16),
            shape((H, H), F32),
            shape((H, H), F32),
        ],
        in_specs=[VMEM, VMEM, VMEM, VMEM, ANY, ANY],
        out_specs=[VMEM] * 5,
        scratch_shapes=[
            pltpu.VMEM((CB, KT, T, T), BF16),
            pltpu.VMEM((CB + 8, T, H), BF16),
            pltpu.VMEM((NC, H), BF16),
            pltpu.VMEM((CB + 8, T, H), F32),
            pltpu.SMEM((KT, 1, CB), I32),
            DMA((5,)),
            DMA,
        ],
        compiler_params=params(),
    )(z0, z0_halo, dz1, weights, columns, tiles)


def lane_row(index):
    return jnp.concatenate([index[0, j : j + 1, :] for j in range(4)], axis=1)


def returned_rows(named, arrived, base, count):
    row = lax.broadcasted_iota(I32, (count, HALO), 0)
    chosen = jnp.where(jnp.broadcast_to(named - base, (count, HALO)) == row, 1.0, 0.0).astype(BF16)
    return dot(chosen, arrived)


WIDE = 512
ROWS = 48


def placed(rows, numbers):
    high, low = rows // T, rows % T
    at = jnp.broadcast_to(high, (ROWS, WIDE)) == lax.broadcasted_iota(I32, (ROWS, WIDE), 0)
    parts = [
        jnp.where(at, jnp.broadcast_to(part.astype(F32), (ROWS, WIDE)), 0.0).astype(BF16)
        for part in (numbers // 64, numbers % 64)
    ]
    lanes = jnp.where(
        jnp.broadcast_to(low, (T, WIDE)) == lax.broadcasted_iota(I32, (T, WIDE), 0), 1.0, 0.0
    ).astype(BF16)
    return dot(jnp.concatenate(parts, axis=0), lanes, NT)


def whole(tables):
    return (tables[:ROWS] * 64.0 + tables[ROWS:]).astype(I32)


def sources(members, pair_send, live):
    nowhere = ROWS * T - 1
    cells = jnp.zeros((2 * ROWS, T), F32)
    for j in range(2):
        for k in range(NC // WIDE):
            cell = lax.broadcasted_iota(I32, (1, WIDE), 1) + k * WIDE
            row = members[0, j : j + 1, k * WIDE : (k + 1) * WIDE]
            cells = cells + placed(jnp.where(cell < live, row, nowhere), cell + 1)
    slots = jnp.zeros((2 * ROWS, T), F32)
    sent = lane_row(pair_send)
    for k in range(HALO // WIDE):
        slot = lax.broadcasted_iota(I32, (1, WIDE), 1) + (NC + k * WIDE)
        slots = slots + placed(sent[:, k * WIDE : (k + 1) * WIDE], slot + 1)
    cells, slots = whole(cells), whole(slots)
    found = jnp.where(cells > 0, cells, jnp.where(slots > 0, slots, NC + HALO + 1)) - 1
    return jnp.minimum(found, NC + HALO)


def gather_block(index, block, source, target, first, width=2, shift=0):
    for g in range(T // UNROLL):
        rows = [
            source[pl.ds(index[block, g * UNROLL + u] * 2 + shift, width), :]
            for u in range(UNROLL)
        ]
        for u in range(UNROLL):
            target[pl.ds((first + g * UNROLL + u) * width, width), :] = rows[u]


NEAR = 8
SIDE = 4
SUM_SEMS = 2 * (NEAR - 1 + SIDE - 1)


class GroupSum:
    def __init__(self, me, grads, near, sides, total, send, recv):
        self.grads, self.near, self.sides, self.total = grads, near, sides, total
        self.send, self.recv = send, recv
        self.rank = me % NEAR
        base = me - self.rank
        self.close = [base + (self.rank + s) % NEAR for s in range(1, NEAR)]
        z, y = me // NEAR % SIDE, me // (NEAR * SIDE)
        self.place = (z, y)
        self.rows = (
            [me + ((z + s) % SIDE - z) * NEAR for s in range(1, SIDE)],
            [me + ((y + s) % SIDE - y) * NEAR * SIDE for s in range(1, SIDE)],
        )
        self.size = near.shape[1]
        self.copies = []

    def greet(self, barrier):
        targets = self.close + self.rows[0] + self.rows[1]
        for target in targets:
            pl.semaphore_signal(barrier, inc=1, device_id=(target,), device_id_type=MESH)
        return len(targets)

    def launch(self, first, moves):
        self.copies = [
            remote(src, dst, self.send.at[first + s], self.recv.at[first + s], target)
            for s, (src, dst, target) in enumerate(moves)
        ]
        for copy in self.copies:
            copy.start()

    def wait(self):
        for copy in self.copies:
            copy.wait()

    def to_near(self):
        size = self.size
        self.launch(
            0,
            [
                (
                    self.grads.at[pl.ds((self.rank + s + 1) % NEAR * size, size)],
                    self.near.at[s],
                    self.close[s],
                )
                for s in range(NEAR - 1)
            ],
        )

    def along(self, side, summed):
        held, place = self.sides[side], self.place[side]
        held[place] = summed
        self.launch(
            NEAR - 1 + side * (SIDE - 1),
            [(held.at[place], held.at[place], target) for target in self.rows[side]],
        )

    def to_z(self):
        self.wait()
        summed = self.grads[pl.ds(self.rank * self.size, self.size), :]
        for s in range(NEAR - 1):
            summed = summed + self.near[s]
        self.along(0, summed)

    def added(self, side):
        self.wait()
        held = self.sides[side]
        return (held[0] + held[1]) + (held[2] + held[3])

    def to_y(self):
        self.along(1, self.added(0))

    def to_all(self):
        mine = pl.ds(self.rank * self.size, self.size)
        self.total[mine, :] = self.added(1)
        self.launch(
            NEAR - 1 + 2 * (SIDE - 1),
            [(self.total.at[mine], self.total.at[mine], target) for target in self.close],
        )


def sum_scratch():
    size = 2 * H // NEAR
    return [
        pltpu.VMEM((2 * H, H), F32),
        pltpu.VMEM((NEAR - 1, size, H), F32),
        pltpu.VMEM((SIDE, size, H), F32),
        pltpu.VMEM((SIDE, size, H), F32),
        pltpu.VMEM((2 * H, H), F32),
        DMA((SUM_SEMS,)),
        DMA((SUM_SEMS,)),
    ]


def coarse_back_kernel(
    n,
    weights,
    count,
    coarse_halo,
    pair_send,
    members,
    m1,
    u1,
    pieces,
    dm,
    dz1_hbm,
    z1_hbm,
    h1_hbm,
    cot_hbm,
    gate_hbm,
    slope_hbm,
    result_hbm,
    low_hbm,
    grads_hbm,
    update_out,
    total_out,
    result_out,
    low_out,
    grads_out,
    arrived,
    rows,
    dz1,
    z1,
    h1,
    cot,
    gate,
    slope,
    cells,
    stage,
    send_out,
    recv_out,
    send_away,
    recv_away,
    table,
    source,
    load_sem,
    store_sem,
    index_sem,
    send_sem,
    recv_sem,
    grads1,
    *sum_refs,
):
    me = lax.axis_index("dom")
    barrier = greet(me, n)
    group = GroupSum(me, grads1, sum_refs[0], sum_refs[1:3], *sum_refs[3:])
    partners = 4 + group.greet(barrier)
    early = loads([(z1_hbm, z1), (dm, rows), (dz1_hbm, dz1)], load_sem)
    later = loads(
        [(h1_hbm, h1), (cot_hbm, cot), (gate_hbm, gate), (slope_hbm, slope)],
        load_sem.at[pl.ds(3, 4)],
    )
    for copy in early + later:
        copy.start()
    targets = [neighbour(me, n, -offset) for offset in OFFSETS]
    grads1[:H, :] = m1[...]
    grads1[H:, :] = u1[...]
    table[...] = sources(members, pair_send, count[0])
    index = pltpu.make_async_copy(table, source, index_sem)
    index.start()
    pl.semaphore_wait(barrier, partners)
    back = [
        remote(
            pieces.at[pl.ds(j * SEND, SEND)],
            arrived.at[pl.ds(j * SEND, SEND)],
            send_sem.at[j],
            recv_sem.at[j],
            targets[j],
        )
        for j in range(4)
    ]
    for copy in back:
        copy.start()
    group.to_near()
    cells[pl.ds(2 * (NC + HALO), 16), :] = jnp.zeros((16, H), F32)
    update_out[...] = jnp.zeros_like(update_out)
    named = lane_row(coarse_halo)
    for copy in early:
        copy.wait()

    def place(i):
        cells[pl.ds(i * 2 * QUAD, QUAD, stride=2), :] = z1[pl.ds(i * QUAD, QUAD), :].astype(F32)

    loop(NC // QUAD, place)

    def exchange_away(shift, sent, received, first):
        copies = []
        for j in range(4):
            loop(
                2,
                lambda t: gather_block(source, FB + 2 * j + t, cells, stage, t * T, 1, shift),
            )
            sent[j] = stage[:SEND, :].astype(BF16)
            copy = remote(
                sent.at[j],
                received.at[j],
                send_sem.at[first + j],
                recv_sem.at[first + j],
                targets[j],
            )
            copy.start()
            copies.append(copy)
        return copies

    index.wait()
    away_out = exchange_away(0, send_out, recv_out, 8)
    group.to_z()
    for copy in back:
        copy.wait()

    def retract(i):
        at = pl.ds(i * QUAD, QUAD)
        parts = [
            rows[pl.ds(i * QUAD + q * SEND, SEND), :]
            + returned_rows(named, arrived[...], i * QUAD + q * SEND, SEND)
            for q in range(2)
        ]
        low = jnp.concatenate(parts, axis=0).astype(BF16)
        cells[pl.ds(i * 2 * QUAD + 1, QUAD, stride=2), :] = dz1[at, :].astype(F32) + dot(
            low, weights[2], NT
        )

    loop(NC // QUAD, retract)
    away = exchange_away(1, send_away, recv_away, 4)
    group.to_y()
    for copy in later:
        copy.wait()
    for shift, copies, received in ((0, away_out, recv_out), (1, away, recv_away)):
        for j in range(4):
            copies[j].wait()
            cells[pl.ds(2 * (NC + j * SEND) + shift, SEND, stride=2), :] = received[j].astype(F32)

    def lift(i):
        loop(4, lambda q: gather_block(source, i * 4 + q, cells, stage, q * T))
        at = pl.ds(i * QUAD, QUAD)
        result_out[at, :] = (
            h1[at, :].astype(F32) + stage[pl.ds(0, QUAD, stride=2), :]
        ).astype(BF16)
        low = (cot[at, :].astype(F32) + stage[pl.ds(1, QUAD, stride=2), :]).astype(BF16)
        low_out[at, :] = low
        update_out[...] += dot(gate[at, :], low, TN)
        grads_out[at, :] = (dot(low, weights[1], NT) * slope[at, :].astype(F32)).astype(BF16)

    group.to_all()
    half = NF // QUAD // 2
    loop(half, lift)
    outs = ((result_out, result_hbm), (low_out, low_hbm), (grads_out, grads_hbm))

    def store(first, sem):
        at = pl.ds(first, NF // 2)
        copies = loads([(src.at[at], dst.at[at]) for src, dst in outs], sem)
        for copy in copies:
            copy.start()
        return copies

    stored = store(0, store_sem.at[pl.ds(0, 3)])
    loop(half, lambda i: lift(i + half))
    stored += store(NF // 2, store_sem.at[pl.ds(3, 3)])
    group.wait()
    total_out[...] = group.total[...]
    for copy in stored:
        copy.wait()


def coarse_back(
    n, number, weights, count, coarse_halo, pair_send, members, m1, u1, pieces, dm, dz1, z1, h1, cot, gate, slope
):
    return pl.pallas_call(
        functools.partial(coarse_back_kernel, n),
        name="coarse_back",
        out_shape=[
            shape((NF, H), BF16),
            shape((NF, H), BF16),
            shape((NF, H), BF16),
            shape((H, H), F32),
            shape((2 * H, H), F32),
        ],
        in_specs=[VMEM, SMEM, VMEM, VMEM, VMEM, VMEM, VMEM] + [ANY] * 8,
        out_specs=[ANY] * 3 + [VMEM] * 2,
        scratch_shapes=[pltpu.VMEM((NF, H), BF16)] * 3
        + [
            pltpu.VMEM((HALO, H), BF16),
            pltpu.VMEM((NC, H), F32),
            pltpu.VMEM((NC, H), BF16),
            pltpu.VMEM((NC, H), BF16),
        ]
        + [pltpu.VMEM((NF, H), BF16)] * 4
        + [
            pltpu.VMEM((2 * (NC + HALO) + 16, H), F32),
            pltpu.VMEM((2 * QUAD, H), F32),
        ]
        + [pltpu.VMEM((4, SEND, H), BF16)] * 4
        + [
            pltpu.VMEM((ROWS, T), I32),
            pltpu.SMEM((ROWS, T), I32),
            DMA((7,)),
            DMA((6,)),
            DMA,
            DMA((12,)),
            DMA((12,)),
        ]
        + sum_scratch(),
        compiler_params=params(collective_id=number, has_side_effects=True),
    )(
        weights,
        count,
        coarse_halo,
        pair_send,
        members,
        m1,
        u1,
        pieces,
        dm,
        dz1,
        z1,
        h1,
        cot,
        gate,
        slope,
    )


def fine_kernel(
    grads,
    values,
    halo,
    columns_hbm,
    tiles,
    result,
    dm_out,
    piece_out,
    message_out,
    result_out,
    buf,
    total,
    held,
    columns,
    index_sem,
    result_sem,
    tile_sem,
):
    index = pltpu.make_async_copy(columns_hbm, columns, index_sem)
    index.start()
    for copy in tile_copies(tiles, buf, tile_sem, 8):
        copy.start()
    taken = pltpu.make_async_copy(result, held, result_sem.at[0])
    taken.start()
    total[...] = jnp.zeros_like(total)
    index.wait()

    def level(i):
        wait_tiles(tiles, buf, tile_sem, i, 4)
        for q in range(4):
            b = i * 4 + q
            spread_row(buf, columns, jnp.transpose(grads[pl.ds(b * T, T), :]), b, total)

    loop(4, level)
    taken.wait()
    passed = pltpu.make_async_copy(held, result_out, result_sem.at[1])
    passed.start()
    loop(4, lambda i: level(i + 4))
    rows_out(total, FB, values, halo, dm_out, piece_out, message_out)
    passed.wait()


def fine_spread(grads, values, halo, columns, tiles, result):
    return pl.pallas_call(
        fine_kernel,
        name="fine_spread",
        out_shape=[
            shape((NF, H), F32),
            shape((HALO, H), BF16),
            shape((H, H), F32),
            shape((NF, H), BF16),
        ],
        in_specs=[VMEM, VMEM, VMEM, ANY, ANY, ANY],
        out_specs=[VMEM, VMEM, VMEM, ANY],
        scratch_shapes=[
            pltpu.VMEM((FB, KT, T, T), BF16),
            pltpu.VMEM((FB + 8, T, H), F32),
            pltpu.VMEM((NF, H), BF16),
            pltpu.SMEM((KT, 1, FB), I32),
            DMA,
            DMA((2,)),
            DMA((8,)),
        ],
        compiler_params=params(),
    )(grads, values, halo, columns, tiles, result)


def fine_back_kernel(
    n,
    weights,
    fine_halo,
    m0,
    u0,
    pieces,
    dm,
    low_hbm,
    grad_out,
    total_out,
    arrived,
    rows,
    low,
    load_sem,
    send_sem,
    recv_sem,
    grads0,
    *sum_refs,
):
    me = lax.axis_index("dom")
    barrier = greet(me, n)
    group = GroupSum(me, grads0, sum_refs[0], sum_refs[1:3], *sum_refs[3:])
    partners = 4 + group.greet(barrier)
    copies = loads([(dm, rows), (low_hbm, low)], load_sem)
    for copy in copies:
        copy.start()
    grads0[:H, :] = m0[...]
    grads0[H:, :] = u0[...]
    named = lane_row(fine_halo)
    pl.semaphore_wait(barrier, partners)
    group.to_near()
    back = [
        remote(
            pieces.at[pl.ds(j * SEND, SEND)],
            arrived.at[pl.ds(j * SEND, SEND)],
            send_sem.at[j],
            recv_sem.at[j],
            neighbour(me, n, -OFFSETS[j]),
        )
        for j in range(4)
    ]
    for copy in back:
        copy.start()
    group.to_z()
    for copy in copies + back:
        copy.wait()

    def retract(i):
        at = pl.ds(i * QUAD, QUAD)
        parts = [
            rows[pl.ds(i * QUAD + q * SEND, SEND), :]
            + returned_rows(named, arrived[...], i * QUAD + q * SEND, SEND)
            for q in range(2)
        ]
        part = jnp.concatenate(parts, axis=0).astype(BF16)
        grad_out[at, :] = (low[at, :].astype(F32) + dot(part, weights[0], NT)).astype(BF16)

    loop(3, retract)
    group.to_y()
    loop(5, lambda i: retract(i + 3))
    group.to_all()
    group.wait()
    total_out[...] = group.total[...]


def fine_back(n, number, weights, fine_halo, m0, u0, pieces, dm, low):
    return pl.pallas_call(
        functools.partial(fine_back_kernel, n),
        name="fine_back",
        out_shape=[shape((NF, H), BF16), shape((2 * H, H), F32)],
        in_specs=[VMEM] * 4 + [ANY] * 3,
        out_specs=[VMEM] * 2,
        scratch_shapes=[
            pltpu.VMEM((HALO, H), BF16),
            pltpu.VMEM((NF, H), F32),
            pltpu.VMEM((NF, H), BF16),
            DMA((2,)),
            DMA((4,)),
            DMA((4,)),
        ]
        + sum_scratch(),
        compiler_params=params(collective_id=number, has_side_effects=True),
    )(weights, fine_halo, m0, u0, pieces, dm, low)


def finish_kernel(grad, fine, coarse, grad_out, totals_out):
    grad_out[...] = grad[...]
    totals_out[pl.ds(0, 2)] = fine[...].reshape(2, H, H)
    totals_out[pl.ds(2, 2)] = coarse[...].reshape(2, H, H)


def finish(grad, fine, coarse):
    return pl.pallas_call(
        finish_kernel,
        name="finish",
        out_shape=[shape(grad.shape, grad.dtype), shape((4, H, H), F32)],
        in_specs=[VMEM] * 3,
        out_specs=[VMEM] * 2,
        compiler_params=params(),
    )(grad, fine, coarse)


def per_device(
    n,
    features,
    cotangent,
    weights,
    fine_tiles,
    fine_columns,
    fine_halo,
    coarse_tiles,
    coarse_columns,
    coarse_halo,
    pair_send,
    members,
    coarse_count,
):
    fine_cols = jnp.transpose(fine_columns, (2, 0, 1))
    coarse_cols = jnp.transpose(coarse_columns, (2, 0, 1))
    h1, gate, slope, halo, z0, z0_halo, dz1 = forward(
        n,
        weights,
        coarse_count,
        features,
        cotangent,
        fine_cols,
        fine_halo,
        coarse_halo,
        pair_send,
        members,
        fine_tiles,
    )
    z1, dm1, piece1, message1, update1 = coarse_level(
        z0, z0_halo, dz1, weights, coarse_cols, coarse_tiles
    )
    result, low, grads, update0, totals1 = coarse_back(
        n,
        1,
        weights,
        coarse_count,
        coarse_halo,
        pair_send,
        members,
        message1,
        update1,
        piece1,
        dm1,
        dz1,
        z1,
        h1,
        cotangent,
        gate,
        slope,
    )
    dm0, piece0, message0, result = fine_spread(
        grads, features, halo, fine_cols, fine_tiles, result
    )
    grad_features, totals0 = fine_back(
        n, 2, weights, fine_halo, message0, update0, piece0, dm0, low
    )
    grad_features, totals = finish(grad_features, totals0, totals1)
    return result, grad_features, totals


def solution(mesh):
    n = mesh.shape["dom"]
    placed = (
        P("dom", None),
        P("dom", None),
        P(),
        P("dom", None, None, None),
        P("dom", None, None),
        P("dom", None, None),
        P("dom", None, None, None),
        P("dom", None, None),
        P("dom", None, None),
        P("dom", None, None),
        P("dom", None, None),
        P("dom"),
    )
    return jax.shard_map(
        functools.partial(per_device, n),
        mesh=mesh,
        in_specs=placed,
        out_specs=(P("dom", None), P("dom", None), P()),
        check_vma=False,
    )
```

```python
import functools

import jax
import jax.numpy as jnp
from jax import lax
from jax.experimental import pallas as pl
from jax.experimental.pallas import tpu as pltpu
from jax.sharding import PartitionSpec as P

MESH = pl.DeviceIdType.MESH
OFFSETS = (1, -1, 8, -8)
F32, BF16, I32 = jnp.float32, jnp.bfloat16, jnp.int32
VMEM = pl.BlockSpec(memory_space=pltpu.VMEM)
SMEM = pl.BlockSpec(memory_space=pltpu.SMEM)
ANY = pl.BlockSpec(memory_space=pl.ANY)
DMA = pltpu.SemaphoreType.DMA
H = 128
T = 128
KT = 12
FB = 32
CB = 20
NF = FB * T
NC = CB * T
SEND = 256
HALO = 4 * SEND
QUAD = 4 * T
UNROLL = 16
GATHER = 32
ORDER = (2, 3, 0, 1)
NN = (((1,), (0,)), ((), ()))
NT = (((1,), (1,)), ((), ()))
TN = (((0,), (0,)), ((), ()))


def dot(a, b, how=NN):
    return lax.dot_general(a, b, how, preferred_element_type=F32)


def shape(dims, dtype):
    return jax.ShapeDtypeStruct(dims, dtype)


def params(mib=56, **more):
    return pltpu.CompilerParams(vmem_limit_bytes=mib * 2**20, **more)


def neighbour(me, n, offset):
    return lax.rem(me + (offset + n), n)


def greet(me, n):
    barrier = pltpu.get_barrier_semaphore()
    for offset in OFFSETS:
        pl.semaphore_signal(
            barrier, inc=1, device_id=(neighbour(me, n, offset),), device_id_type=MESH
        )
    return barrier


def remote(src, dst, send_sem, recv_sem, target):
    return pltpu.make_async_remote_copy(
        src_ref=src,
        dst_ref=dst,
        send_sem=send_sem,
        recv_sem=recv_sem,
        device_id=(target,),
        device_id_type=MESH,
    )


def index_copies(pairs, sem):
    copies = []
    for src, dst in pairs:
        width = src.shape[2]
        for j in range(src.shape[1]):
            copies.append((src.at[0, j], dst.at[pl.ds(j * width, width)]))
    return [pltpu.make_async_copy(a, b, sem.at[i]) for i, (a, b) in enumerate(copies)]


def loop(count, body, unroll=1):
    def step(i, carry):
        body(i)
        return carry

    lax.fori_loop(0, count, step, 0, unroll=unroll)


def gather_rows(index, first, source, target, count, step=1, shift=0):
    def body(i):
        base = pl.multiple_of(i * GATHER, GATHER)
        rows = [
            source[pl.ds(index[first + base + u] * step + shift, 1), :] for u in range(GATHER)
        ]
        for u in range(GATHER):
            target[pl.ds(base + u, 1), :] = rows[u]

    loop(count // GATHER, body)


def block_row(tiles, columns, blocks, b):
    lhs = jnp.concatenate([tiles[b, k] for k in range(KT)], axis=1)
    rhs = jnp.concatenate([blocks[columns[k, 0, b]] for k in range(KT)], axis=0)
    return dot(lhs, rhs)


def spread_row(tiles, columns, grads_t, b, total):
    for k in range(KT):
        c = columns[k, 0, b]
        total[c] = total[c] + dot(grads_t, tiles[b, k])


def tile_copies(source, buffer, sem, count):
    size = source.shape[0] // count
    return [
        pltpu.make_async_copy(
            source.at[pl.ds(i * size, size)], buffer.at[pl.ds(i * size, size)], sem.at[i]
        )
        for i in range(count)
    ]


def wait_tiles(source, buffer, sem, i, size):
    pltpu.make_async_copy(
        source.at[pl.ds(i * size, size)], buffer.at[pl.ds(i * size, size)], sem.at[i]
    ).wait()


def loads(pairs, sem):
    return [pltpu.make_async_copy(src, dst, sem.at[i]) for i, (src, dst) in enumerate(pairs)]


def lane_row(index):
    return jnp.concatenate([index[0, j : j + 1, :] for j in range(4)], axis=1)


def returned_rows(named, arrived, base, count):
    row = lax.broadcasted_iota(I32, (count, HALO), 0)
    chosen = jnp.where(jnp.broadcast_to(named - base, (count, HALO)) == row, 1.0, 0.0).astype(BF16)
    return dot(chosen, arrived)


WIDE = 512
ROWS = 48


def placed(rows, numbers):
    high, low = rows // T, rows % T
    at = jnp.broadcast_to(high, (ROWS, WIDE)) == lax.broadcasted_iota(I32, (ROWS, WIDE), 0)
    parts = [
        jnp.where(at, jnp.broadcast_to(part.astype(F32), (ROWS, WIDE)), 0.0).astype(BF16)
        for part in (numbers // 64, numbers % 64)
    ]
    lanes = jnp.where(
        jnp.broadcast_to(low, (T, WIDE)) == lax.broadcasted_iota(I32, (T, WIDE), 0), 1.0, 0.0
    ).astype(BF16)
    return dot(jnp.concatenate(parts, axis=0), lanes, NT)


def whole(tables):
    return (tables[:ROWS] * 64.0 + tables[ROWS:]).astype(I32)


def sources(members, pair_send, live):
    nowhere = ROWS * T - 1
    cells = jnp.zeros((2 * ROWS, T), F32)
    for j in range(2):
        for k in range(NC // WIDE):
            cell = lax.broadcasted_iota(I32, (1, WIDE), 1) + k * WIDE
            row = members[0, j : j + 1, k * WIDE : (k + 1) * WIDE]
            cells = cells + placed(jnp.where(cell < live, row, nowhere), cell + 1)
    slots = jnp.zeros((2 * ROWS, T), F32)
    sent = lane_row(pair_send)
    for k in range(HALO // WIDE):
        slot = lax.broadcasted_iota(I32, (1, WIDE), 1) + (NC + k * WIDE)
        slots = slots + placed(sent[:, k * WIDE : (k + 1) * WIDE], slot + 1)
    cells, slots = whole(cells), whole(slots)
    found = jnp.where(cells > 0, cells, jnp.where(slots > 0, slots, NC + HALO + 1)) - 1
    return jnp.minimum(found, NC + HALO)


def forward_kernel(
    n,
    weights,
    count,
    member_rows,
    pair_rows,
    values_hbm,
    cot_hbm,
    columns_hbm,
    fine_halo,
    coarse_halo,
    pair_send,
    members,
    tiles,
    h1_hbm,
    gate_hbm,
    slope_hbm,
    halo_hbm,
    z0_hbm,
    z0_halo_hbm,
    dz1_hbm,
    table,
    values,
    cot,
    h1,
    gates,
    slopes,
    z0_rows,
    dz1_rows,
    buf,
    ext,
    rows32,
    pairs,
    cells,
    stage,
    send_fine,
    recv_fine,
    send_cot,
    recv_cot,
    send_pair,
    recv_pair,
    send_coarse,
    recv_coarse,
    s_fine,
    s_coarse,
    s_pair,
    s_members,
    columns,
    load_sem,
    store_sem,
    tile_sem,
    index_sem,
    send_sem,
    recv_sem,
):
    me = lax.axis_index("dom")
    barrier = greet(me, n)
    taken = loads([(values_hbm, values), (cot_hbm, cot)], load_sem)
    index = index_copies(
        [(fine_halo, s_fine), (coarse_halo, s_coarse), (pair_send, s_pair), (members, s_members)],
        index_sem,
    )
    index.append(pltpu.make_async_copy(columns_hbm, columns, index_sem.at[14]))
    for copy in taken[:1] + index + taken[1:]:
        copy.start()
    for copy in tile_copies(tiles, buf, tile_sem, 8):
        copy.start()
    taken[0].wait()

    def widen(i):
        at = pl.ds(i * QUAD, QUAD)
        rows32[at, :] = values[at, :].astype(F32)

    loop(NF // QUAD, widen)
    for copy in index:
        copy.wait()
    targets = [neighbour(me, n, offset) for offset in OFFSETS]

    def exchange(index, source, sent, received, first, step=1, shift=0, ready=None):
        copies = [None] * 4
        for j in ORDER:
            gather_rows(index, j * SEND, source, stage, SEND, step, shift)
            sent[j] = stage[...].astype(BF16)
            if ready is not None and j == ORDER[0]:
                pl.semaphore_wait(ready, 4)
            copy = remote(
                sent.at[j],
                received.at[j],
                send_sem.at[first + j],
                recv_sem.at[first + j],
                targets[j],
            )
            copy.start()
            copies[j] = copy
        return copies

    fine = exchange(s_fine, rows32, send_fine, recv_fine, 0, ready=barrier)

    def project(i):
        at = pl.ds(i * QUAD, QUAD)
        ext[pl.ds(i * 4, 4)] = dot(values[at, :], weights[0]).astype(BF16).reshape(4, T, H)

    loop(NF // QUAD, project)
    taken[1].wait()

    def place_cot(i):
        pairs[pl.ds(i * 2 * QUAD + 1, QUAD, stride=2), :] = cot[pl.ds(i * QUAD, QUAD), :].astype(F32)

    loop(NF // QUAD, place_cot)
    paired_cot = exchange(s_pair, pairs, send_cot, recv_cot, 12, 2, 1)
    table[...] = sources(member_rows, pair_rows, count[0])
    pairs[pl.ds(2 * NF, HALO, stride=2), :] = jnp.zeros((HALO, H), F32)
    for j in range(4):
        fine[j].wait()
        ext[pl.ds(FB + 2 * j, 2)] = dot(recv_fine[j], weights[0]).astype(BF16).reshape(2, T, H)

    def level(i):
        wait_tiles(tiles, buf, tile_sem, i, 4)
        parts = []
        for q in range(4):
            b = i * 4 + q
            parts.append(block_row(buf, columns, ext, b))
        summed = jnp.concatenate(parts, axis=0)
        sigma = jax.nn.sigmoid(summed)
        gate = (summed * sigma).astype(BF16)
        at = pl.ds(i * QUAD, QUAD)
        gates[at, :] = gate
        slopes[at, :] = (sigma * (1.0 + summed * (1.0 - sigma))).astype(BF16)
        out = (values[at, :].astype(F32) + dot(gate, weights[1])).astype(BF16)
        h1[at, :] = out
        pairs[pl.ds(i * 2 * QUAD, QUAD, stride=2), :] = out.astype(F32)

    loop(8, level)
    paired = exchange(s_pair, pairs, send_pair, recv_pair, 4, 2, 0)
    outs = [(h1, h1_hbm), (gates, gate_hbm), (slopes, slope_hbm), (recv_fine, halo_hbm)]
    stored = loads(outs, store_sem)
    for copy in stored:
        copy.start()
    for j in range(4):
        paired_cot[j].wait()
        pairs[pl.ds(2 * (NF + j * SEND) + 1, SEND, stride=2), :] = recv_cot[j].astype(F32)

    def pool(i):
        base = pl.multiple_of(i * 2 * GATHER, 2 * GATHER)
        for half in range(0, 2 * GATHER, GATHER):
            at = range(half, half + GATHER)
            first = [pairs[pl.ds(s_members[base + u] * 2, 2), :] for u in at]
            second = [pairs[pl.ds(s_members[NC + base + u] * 2, 2), :] for u in at]
            for u in at:
                cells[pl.ds((base + u) * 2, 2), :] = first[u - half] + second[u - half]

    loop(NC // (2 * GATHER), pool)
    live = count[0]
    for copy in paired:
        copy.wait()
    named = jnp.concatenate([table[FB + t : FB + t + 1, :] for t in range(8)], axis=1)

    def pooled(i):
        at = pl.ds(i * QUAD, QUAD)
        row = lax.broadcasted_iota(I32, (QUAD, H), 0) + i * QUAD
        received = jnp.concatenate(
            [
                returned_rows(named, recv_pair[...].reshape(HALO, H), i * QUAD + q * SEND, SEND)
                for q in range(2)
            ],
            axis=0,
        )
        z0 = cells[pl.ds(i * 2 * QUAD, QUAD, stride=2), :] + received
        z0 = jnp.where(row < live, z0, 0.0).astype(BF16)
        z0_rows[at, :] = z0
        rows32[at, :] = z0.astype(F32)

    loop(NC // QUAD, pooled)
    coarse = exchange(s_coarse, rows32, send_coarse, recv_coarse, 8)
    stored += loads([(z0_rows, z0_hbm)], store_sem.at[pl.ds(4, 1)])
    stored[-1].start()

    def pooled_cot(i):
        at = pl.ds(i * QUAD, QUAD)
        row = lax.broadcasted_iota(I32, (QUAD, H), 0) + i * QUAD
        dz1_rows[at, :] = jnp.where(
            row < live, cells[pl.ds(i * 2 * QUAD + 1, QUAD, stride=2), :], 0.0
        ).astype(BF16)

    loop(NC // QUAD, pooled_cot)
    stored += loads([(dz1_rows, dz1_hbm)], store_sem.at[pl.ds(5, 1)])
    stored[-1].start()
    for copy in coarse:
        copy.wait()
    stored += loads([(recv_coarse, z0_halo_hbm)], store_sem.at[pl.ds(6, 1)])
    stored[-1].start()
    for copy in stored:
        copy.wait()


def forward(n, weights, count, values, cot, columns, fine_halo, coarse_halo, pair_send, members, tiles):
    return pl.pallas_call(
        functools.partial(forward_kernel, n),
        name="forward",
        out_shape=[
            shape((NF, H), BF16),
            shape((NF, H), BF16),
            shape((NF, H), BF16),
            shape((4, SEND, H), BF16),
            shape((NC, H), BF16),
            shape((4, SEND, H), BF16),
            shape((NC, H), BF16),
            shape((ROWS, T), I32),
        ],
        in_specs=[VMEM, SMEM, VMEM, VMEM] + [ANY] * 8,
        out_specs=[ANY] * 7 + [VMEM],
        scratch_shapes=[pltpu.VMEM((NF, H), BF16)] * 5
        + [pltpu.VMEM((NC, H), BF16)] * 2
        + [
            pltpu.VMEM((FB, KT, T, T), BF16),
            pltpu.VMEM((FB + 8, T, H), BF16),
            pltpu.VMEM((NF, H), F32),
            pltpu.VMEM((2 * (NF + HALO), H), F32),
            pltpu.VMEM((2 * NC, H), F32),
            pltpu.VMEM((SEND, H), F32),
        ]
        + [pltpu.VMEM((4, SEND, H), BF16)] * 8
        + [
            pltpu.SMEM((HALO,), I32),
            pltpu.SMEM((HALO,), I32),
            pltpu.SMEM((HALO,), I32),
            pltpu.SMEM((2 * NC,), I32),
            pltpu.SMEM((KT, 1, FB), I32),
            DMA((2,)),
            DMA((7,)),
            DMA((8,)),
            DMA((15,)),
            DMA((16,)),
            DMA((16,)),
        ],
        compiler_params=params(collective_id=0, has_side_effects=True),
    )(
        weights,
        count,
        members,
        pair_send,
        values,
        cot,
        columns,
        fine_halo,
        coarse_halo,
        pair_send,
        members,
        tiles,
    )


def rows_out(total, blocks, own_values, halo_values, own, own_hbm, sem, halo_ref, message_ref):
    def place(c):
        part = total[c]
        at = pl.ds(c * T, T)
        own[at, :] = jnp.transpose(part)
        message_ref[...] += dot(part.astype(BF16), own_values[at, :])

    def halo(c):
        part = total[blocks + c]
        halo_ref[pl.ds(c * T, T), :] = jnp.transpose(part).astype(BF16)
        message_ref[...] += dot(part.astype(BF16), halo_values[c // 2, pl.ds(c % 2 * T, T), :])

    message_ref[...] = jnp.zeros_like(message_ref)
    quarter = blocks // 4
    copies = []
    for part in range(4):
        loop(quarter, lambda c: place(part * quarter + c), quarter)
        at = pl.ds(part * quarter * T, quarter * T)
        copies.append(pltpu.make_async_copy(own.at[at], own_hbm.at[at], sem.at[part]))
        copies[-1].start()
    loop(8, halo, 8)
    message_ref[...] = jnp.transpose(message_ref[...])
    for copy in copies:
        copy.wait()


def coarse_kernel(
    z0,
    z0_halo,
    dz1,
    weights,
    columns_hbm,
    tiles,
    z1_out,
    dm_hbm,
    piece_out,
    message_out,
    update_out,
    dm,
    dm_sem,
    buf,
    ext,
    gates,
    total,
    columns,
    tile_sem,
    index_sem,
):
    index = pltpu.make_async_copy(columns_hbm, columns, index_sem)
    index.start()
    for copy in tile_copies(tiles, buf, tile_sem, 5):
        copy.start()

    def project(i):
        part = z0[pl.ds(i * QUAD, QUAD), :]
        ext[pl.ds(i * 4, 4)] = dot(part, weights[2]).astype(BF16).reshape(4, T, H)

    loop(CB // 4, project)
    ext[pl.ds(CB, 8)] = dot(z0_halo[...].reshape(HALO, H), weights[2]).astype(BF16).reshape(8, T, H)
    total[...] = jnp.zeros_like(total)
    index.wait()

    def level(i):
        wait_tiles(tiles, buf, tile_sem, i, 4)
        parts = []
        for q in range(4):
            b = i * 4 + q
            parts.append(block_row(buf, columns, ext, b))
        summed = jnp.concatenate(parts, axis=0)
        sigma = jax.nn.sigmoid(summed)
        gate = (summed * sigma).astype(BF16)
        at = pl.ds(i * QUAD, QUAD)
        gates[at, :] = gate
        z1_out[at, :] = (z0[at, :].astype(F32) + dot(gate, weights[3])).astype(BF16)
        slope = sigma * (1.0 + summed * (1.0 - sigma))
        grads = (dot(dz1[at, :], weights[3], NT) * slope).astype(BF16)
        for q in range(4):
            b = i * 4 + q
            grads_t = jnp.transpose(grads[q * T : (q + 1) * T, :])
            spread_row(buf, columns, grads_t, b, total)

    loop(CB // 4, level)
    update_out[...] = dot(gates[...], dz1[...], TN)
    rows_out(total, CB, z0, z0_halo, dm, dm_hbm, dm_sem, piece_out, message_out)


def coarse_level(z0, z0_halo, dz1, weights, columns, tiles):
    return pl.pallas_call(
        coarse_kernel,
        name="coarse_level",
        out_shape=[
            shape((NC, H), BF16),
            shape((NC, H), F32),
            shape((HALO, H), BF16),
            shape((H, H), F32),
            shape((H, H), F32),
        ],
        in_specs=[VMEM, VMEM, VMEM, VMEM, ANY, ANY],
        out_specs=[VMEM, ANY, VMEM, VMEM, VMEM],
        scratch_shapes=[
            pltpu.VMEM((NC, H), F32),
            DMA((4,)),
            pltpu.VMEM((CB, KT, T, T), BF16),
            pltpu.VMEM((CB + 8, T, H), BF16),
            pltpu.VMEM((NC, H), BF16),
            pltpu.VMEM((CB + 8, T, H), F32),
            pltpu.SMEM((KT, 1, CB), I32),
            DMA((5,)),
            DMA,
        ],
        compiler_params=params(),
    )(z0, z0_halo, dz1, weights, columns, tiles)


def gather_block(index, block, source, target, first, width=2, shift=0):
    for g in range(T // UNROLL):
        rows = [
            source[pl.ds(index[block, g * UNROLL + u] * 2 + shift, width), :]
            for u in range(UNROLL)
        ]
        for u in range(UNROLL):
            target[pl.ds((first + g * UNROLL + u) * width, width), :] = rows[u]


NEAR = 8
SIDE = 4
SUM_SEMS = 2 * (NEAR - 1 + SIDE - 1)


class GroupSum:
    def __init__(self, me, grads, near, sides, total, send, recv):
        self.grads, self.near, self.sides, self.total = grads, near, sides, total
        self.send, self.recv = send, recv
        self.rank = me % NEAR
        base = me - self.rank
        self.close = [base + (self.rank + s) % NEAR for s in range(1, NEAR)]
        z, y = me // NEAR % SIDE, me // (NEAR * SIDE)
        self.place = (z, y)
        self.rows = (
            [me + ((z + s) % SIDE - z) * NEAR for s in range(1, SIDE)],
            [me + ((y + s) % SIDE - y) * NEAR * SIDE for s in range(1, SIDE)],
        )
        self.size = near.shape[1]
        self.copies = []

    def greet(self, barrier):
        targets = self.close + self.rows[0] + self.rows[1]
        for target in targets:
            pl.semaphore_signal(barrier, inc=1, device_id=(target,), device_id_type=MESH)
        return len(targets)

    def launch(self, first, moves):
        self.copies = [
            remote(src, dst, self.send.at[first + s], self.recv.at[first + s], target)
            for s, (src, dst, target) in enumerate(moves)
        ]
        for copy in self.copies:
            copy.start()

    def wait(self):
        for copy in self.copies:
            copy.wait()

    def to_near(self):
        size = self.size
        self.launch(
            0,
            [
                (
                    self.grads.at[pl.ds((self.rank + s + 1) % NEAR * size, size)],
                    self.near.at[s],
                    self.close[s],
                )
                for s in range(NEAR - 1)
            ],
        )

    def along(self, side, summed):
        held, place = self.sides[side], self.place[side]
        held[place] = summed
        self.launch(
            NEAR - 1 + side * (SIDE - 1),
            [(held.at[place], held.at[place], target) for target in self.rows[side]],
        )

    def to_z(self):
        self.wait()
        summed = self.grads[pl.ds(self.rank * self.size, self.size), :]
        for s in range(NEAR - 1):
            summed = summed + self.near[s]
        self.along(0, summed)

    def added(self, side):
        self.wait()
        held = self.sides[side]
        return (held[0] + held[1]) + (held[2] + held[3])

    def to_y(self):
        self.along(1, self.added(0))

    def to_all(self):
        mine = pl.ds(self.rank * self.size, self.size)
        self.total[mine, :] = self.added(1)
        self.launch(
            NEAR - 1 + 2 * (SIDE - 1),
            [(self.total.at[mine], self.total.at[mine], target) for target in self.close],
        )


def sum_scratch():
    size = 2 * H // NEAR
    return [
        pltpu.VMEM((2 * H, H), F32),
        pltpu.VMEM((NEAR - 1, size, H), F32),
        pltpu.VMEM((SIDE, size, H), F32),
        pltpu.VMEM((SIDE, size, H), F32),
        pltpu.VMEM((2 * H, H), F32),
        DMA((SUM_SEMS,)),
        DMA((SUM_SEMS,)),
    ]


def coarse_back_kernel(
    n,
    weights,
    coarse_halo,
    m1,
    u1,
    table,
    pieces,
    dm,
    dz1_hbm,
    z1_hbm,
    h1_hbm,
    cot_hbm,
    gate_hbm,
    slope_hbm,
    result_hbm,
    low_hbm,
    grads_hbm,
    update_out,
    total_out,
    result_out,
    low_out,
    grads_out,
    arrived,
    rows,
    dz1,
    z1,
    h1,
    cot,
    gate,
    slope,
    cells,
    stage,
    even,
    odd,
    send_out,
    recv_out,
    send_away,
    recv_away,
    source,
    load_sem,
    store_sem,
    index_sem,
    send_sem,
    recv_sem,
    grads1,
    *sum_refs,
):
    me = lax.axis_index("dom")
    barrier = greet(me, n)
    group = GroupSum(me, grads1, sum_refs[0], sum_refs[1:3], *sum_refs[3:])
    partners = 4 + group.greet(barrier)
    early = loads([(z1_hbm, z1), (dm, rows), (dz1_hbm, dz1)], load_sem)
    later = loads(
        [(h1_hbm, h1), (cot_hbm, cot), (gate_hbm, gate), (slope_hbm, slope)],
        load_sem.at[pl.ds(3, 4)],
    )
    for copy in early + later:
        copy.start()
    targets = [neighbour(me, n, -offset) for offset in OFFSETS]
    grads1[:H, :] = m1[...]
    grads1[H:, :] = u1[...]
    index = pltpu.make_async_copy(table, source, index_sem)
    index.start()
    pl.semaphore_wait(barrier, partners)
    back = [
        remote(
            pieces.at[pl.ds(j * SEND, SEND)],
            arrived.at[pl.ds(j * SEND, SEND)],
            send_sem.at[j],
            recv_sem.at[j],
            targets[j],
        )
        for j in ORDER
    ]
    for copy in back:
        copy.start()
    group.to_near()
    cells[pl.ds(2 * (NC + HALO), 16), :] = jnp.zeros((16, H), F32)
    update_out[...] = jnp.zeros_like(update_out)
    named = lane_row(coarse_halo)
    for copy in early:
        copy.wait()

    def place(i):
        cells[pl.ds(i * 2 * QUAD, QUAD, stride=2), :] = z1[pl.ds(i * QUAD, QUAD), :].astype(F32)

    loop(NC // QUAD, place)

    def exchange_away(shift, sent, received, first):
        copies = [None] * 4
        for j in ORDER:
            loop(
                2,
                lambda t: gather_block(source, FB + 2 * j + t, cells, stage, t * T, 1, shift),
            )
            sent[j] = stage[...].astype(BF16)
            copy = remote(
                sent.at[j],
                received.at[j],
                send_sem.at[first + j],
                recv_sem.at[first + j],
                targets[j],
            )
            copy.start()
            copies[j] = copy
        return copies

    index.wait()
    away_out = exchange_away(0, send_out, recv_out, 8)
    group.to_z()
    for copy in back:
        copy.wait()

    def retract(i):
        at = pl.ds(i * QUAD, QUAD)
        parts = [
            rows[pl.ds(i * QUAD + q * SEND, SEND), :]
            + returned_rows(named, arrived[...], i * QUAD + q * SEND, SEND)
            for q in range(2)
        ]
        low = jnp.concatenate(parts, axis=0).astype(BF16)
        cells[pl.ds(i * 2 * QUAD + 1, QUAD, stride=2), :] = dz1[at, :].astype(F32) + dot(
            low, weights[2], NT
        )

    loop(NC // QUAD, retract)
    away = exchange_away(1, send_away, recv_away, 4)
    group.to_y()
    for copy in later:
        copy.wait()
    for shift, copies, received in ((0, away_out, recv_out), (1, away, recv_away)):
        for j in range(4):
            copies[j].wait()
            cells[pl.ds(2 * (NC + j * SEND) + shift, SEND, stride=2), :] = received[j].astype(F32)

    def lift(b, lifted):
        at = pl.ds(b * T, T)
        result_out[at, :] = (h1[at, :].astype(F32) + lifted[pl.ds(0, T, stride=2), :]).astype(BF16)
        low = (cot[at, :].astype(F32) + lifted[pl.ds(1, T, stride=2), :]).astype(BF16)
        low_out[at, :] = low
        update_out[...] += dot(gate[at, :], low, TN)
        grads_out[at, :] = (dot(low, weights[1], NT) * slope[at, :].astype(F32)).astype(BF16)

    def lift_two(i):
        gather_block(source, 2 * i + 1, cells, odd, 0)
        lift(2 * i, even)
        gather_block(source, (2 * i + 2) % FB, cells, even, 0)
        lift(2 * i + 1, odd)

    group.to_all()
    gather_block(source, 0, cells, even, 0)
    half = FB // 4
    loop(half, lift_two)
    outs = ((result_out, result_hbm), (low_out, low_hbm), (grads_out, grads_hbm))

    def store(first, sem):
        at = pl.ds(first, NF // 2)
        copies = loads([(src.at[at], dst.at[at]) for src, dst in outs], sem)
        for copy in copies:
            copy.start()
        return copies

    stored = store(0, store_sem.at[pl.ds(0, 3)])
    loop(half, lambda i: lift_two(i + half))
    stored += store(NF // 2, store_sem.at[pl.ds(3, 3)])
    group.wait()
    total_out[...] = group.total[...]
    for copy in stored:
        copy.wait()


def coarse_back(
    n, number, weights, coarse_halo, m1, u1, table, pieces, dm, dz1, z1, h1, cot, gate, slope
):
    return pl.pallas_call(
        functools.partial(coarse_back_kernel, n),
        name="coarse_back",
        out_shape=[
            shape((NF, H), BF16),
            shape((NF, H), BF16),
            shape((NF, H), BF16),
            shape((H, H), F32),
            shape((2 * H, H), F32),
        ],
        in_specs=[VMEM] * 4 + [ANY] * 9,
        out_specs=[ANY] * 3 + [VMEM] * 2,
        scratch_shapes=[pltpu.VMEM((NF, H), BF16)] * 3
        + [
            pltpu.VMEM((HALO, H), BF16),
            pltpu.VMEM((NC, H), F32),
            pltpu.VMEM((NC, H), BF16),
            pltpu.VMEM((NC, H), BF16),
        ]
        + [pltpu.VMEM((NF, H), BF16)] * 4
        + [
            pltpu.VMEM((2 * (NC + HALO) + 16, H), F32),
            pltpu.VMEM((SEND, H), F32),
            pltpu.VMEM((2 * T, H), F32),
            pltpu.VMEM((2 * T, H), F32),
        ]
        + [pltpu.VMEM((4, SEND, H), BF16)] * 4
        + [
            pltpu.SMEM((ROWS, T), I32),
            DMA((7,)),
            DMA((6,)),
            DMA,
            DMA((12,)),
            DMA((12,)),
        ]
        + sum_scratch(),
        compiler_params=params(collective_id=number, has_side_effects=True),
    )(
        weights,
        coarse_halo,
        m1,
        u1,
        table,
        pieces,
        dm,
        dz1,
        z1,
        h1,
        cot,
        gate,
        slope,
    )


def fine_kernel(
    grads_hbm,
    values_hbm,
    halo_hbm,
    columns_hbm,
    tiles,
    result_in,
    dm_hbm,
    piece_out,
    message_out,
    result_out,
    grads,
    values,
    halo,
    result,
    dm,
    buf,
    total,
    columns,
    load_sem,
    store_sem,
    tile_sem,
):
    first = loads([(columns_hbm, columns), (grads_hbm, grads)], load_sem)
    for copy in first:
        copy.start()
    for copy in tile_copies(tiles, buf, tile_sem, 8):
        copy.start()
    later = loads(
        [(values_hbm, values), (halo_hbm, halo), (result_in, result)], load_sem.at[pl.ds(2, 3)]
    )
    for copy in later:
        copy.start()
    total[...] = jnp.zeros_like(total)
    for copy in first:
        copy.wait()

    def level(i):
        wait_tiles(tiles, buf, tile_sem, i, 4)
        for q in range(4):
            b = i * 4 + q
            spread_row(buf, columns, jnp.transpose(grads[pl.ds(b * T, T), :]), b, total)

    loop(6, level)
    for copy in later:
        copy.wait()
    passed = pltpu.make_async_copy(result, result_out, store_sem.at[4])
    passed.start()
    loop(2, lambda i: level(i + 6))
    rows_out(total, FB, values, halo, dm, dm_hbm, store_sem, piece_out, message_out)
    passed.wait()


def fine_spread(grads, values, halo, columns, tiles, result):
    return pl.pallas_call(
        fine_kernel,
        name="fine_spread",
        out_shape=[
            shape((NF, H), F32),
            shape((HALO, H), BF16),
            shape((H, H), F32),
            shape((NF, H), BF16),
        ],
        in_specs=[ANY] * 6,
        out_specs=[ANY, VMEM, VMEM, ANY],
        scratch_shapes=[
            pltpu.VMEM((NF, H), BF16),
            pltpu.VMEM((NF, H), BF16),
            pltpu.VMEM((4, SEND, H), BF16),
            pltpu.VMEM((NF, H), BF16),
            pltpu.VMEM((NF, H), F32),
            pltpu.VMEM((FB, KT, T, T), BF16),
            pltpu.VMEM((FB + 8, T, H), F32),
            pltpu.SMEM((KT, 1, FB), I32),
            DMA((5,)),
            DMA((5,)),
            DMA((8,)),
        ],
        compiler_params=params(),
    )(grads, values, halo, columns, tiles, result)


def fine_back_kernel(
    n,
    weights,
    fine_halo,
    m0,
    u0,
    pieces,
    dm,
    low_hbm,
    grad_out,
    total_out,
    arrived,
    rows,
    low,
    load_sem,
    send_sem,
    recv_sem,
    grads0,
    *sum_refs,
):
    me = lax.axis_index("dom")
    barrier = greet(me, n)
    group = GroupSum(me, grads0, sum_refs[0], sum_refs[1:3], *sum_refs[3:])
    partners = 4 + group.greet(barrier)
    copies = loads([(dm, rows), (low_hbm, low)], load_sem)
    for copy in copies:
        copy.start()
    grads0[:H, :] = m0[...]
    grads0[H:, :] = u0[...]
    named = lane_row(fine_halo)
    pl.semaphore_wait(barrier, partners)
    group.to_near()
    back = [
        remote(
            pieces.at[pl.ds(j * SEND, SEND)],
            arrived.at[pl.ds(j * SEND, SEND)],
            send_sem.at[j],
            recv_sem.at[j],
            neighbour(me, n, -OFFSETS[j]),
        )
        for j in ORDER
    ]
    for copy in back:
        copy.start()
    group.to_z()
    for copy in copies + back:
        copy.wait()

    def retract(i):
        at = pl.ds(i * QUAD, QUAD)
        parts = [
            rows[pl.ds(i * QUAD + q * SEND, SEND), :]
            + returned_rows(named, arrived[...], i * QUAD + q * SEND, SEND)
            for q in range(2)
        ]
        part = jnp.concatenate(parts, axis=0).astype(BF16)
        grad_out[at, :] = (low[at, :].astype(F32) + dot(part, weights[0], NT)).astype(BF16)

    loop(3, retract)
    group.to_y()
    loop(5, lambda i: retract(i + 3))
    group.to_all()
    group.wait()
    total_out[...] = group.total[...]


def fine_back(n, number, weights, fine_halo, m0, u0, pieces, dm, low):
    return pl.pallas_call(
        functools.partial(fine_back_kernel, n),
        name="fine_back",
        out_shape=[shape((NF, H), BF16), shape((2 * H, H), F32)],
        in_specs=[VMEM] * 4 + [ANY] * 3,
        out_specs=[VMEM] * 2,
        scratch_shapes=[
            pltpu.VMEM((HALO, H), BF16),
            pltpu.VMEM((NF, H), F32),
            pltpu.VMEM((NF, H), BF16),
            DMA((2,)),
            DMA((4,)),
            DMA((4,)),
        ]
        + sum_scratch(),
        compiler_params=params(collective_id=number, has_side_effects=True),
    )(weights, fine_halo, m0, u0, pieces, dm, low)


def finish_kernel(grad, fine, coarse, grad_out, totals_out):
    grad_out[...] = grad[...]
    totals_out[pl.ds(0, 2)] = fine[...].reshape(2, H, H)
    totals_out[pl.ds(2, 2)] = coarse[...].reshape(2, H, H)


def finish(grad, fine, coarse):
    return pl.pallas_call(
        finish_kernel,
        name="finish",
        out_shape=[shape(grad.shape, grad.dtype), shape((4, H, H), F32)],
        in_specs=[VMEM] * 3,
        out_specs=[VMEM] * 2,
        compiler_params=params(),
    )(grad, fine, coarse)


def per_device(
    n,
    features,
    cotangent,
    weights,
    fine_tiles,
    fine_columns,
    fine_halo,
    coarse_tiles,
    coarse_columns,
    coarse_halo,
    pair_send,
    members,
    coarse_count,
):
    fine_cols = jnp.transpose(fine_columns, (2, 0, 1))
    coarse_cols = jnp.transpose(coarse_columns, (2, 0, 1))
    h1, gate, slope, halo, z0, z0_halo, dz1, table = forward(
        n,
        weights,
        coarse_count,
        features,
        cotangent,
        fine_cols,
        fine_halo,
        coarse_halo,
        pair_send,
        members,
        fine_tiles,
    )
    z1, dm1, piece1, message1, update1 = coarse_level(
        z0, z0_halo, dz1, weights, coarse_cols, coarse_tiles
    )
    result, low, grads, update0, totals1 = coarse_back(
        n,
        1,
        weights,
        coarse_halo,
        message1,
        update1,
        table,
        piece1,
        dm1,
        dz1,
        z1,
        h1,
        cotangent,
        gate,
        slope,
    )
    dm0, piece0, message0, result = fine_spread(
        grads, features, halo, fine_cols, fine_tiles, result
    )
    grad_features, totals0 = fine_back(
        n, 2, weights, fine_halo, message0, update0, piece0, dm0, low
    )
    grad_features, totals = finish(grad_features, totals0, totals1)
    return result, grad_features, totals


def solution(mesh):
    n = mesh.shape["dom"]
    placed = (
        P("dom", None),
        P("dom", None),
        P(),
        P("dom", None, None, None),
        P("dom", None, None),
        P("dom", None, None),
        P("dom", None, None, None),
        P("dom", None, None),
        P("dom", None, None),
        P("dom", None, None),
        P("dom", None, None),
        P("dom"),
    )
    return jax.shard_map(
        functools.partial(per_device, n),
        mesh=mesh,
        in_specs=placed,
        out_specs=(P("dom", None), P("dom", None), P()),
        check_vma=False,
    )
```

```python
import functools

import jax
import jax.numpy as jnp
from jax import lax
from jax.experimental import pallas as pl
from jax.experimental.pallas import tpu as pltpu
from jax.sharding import PartitionSpec as P

MESH = pl.DeviceIdType.MESH
OFFSETS = (1, -1, 8, -8)
F32, BF16, I32 = jnp.float32, jnp.bfloat16, jnp.int32
VMEM = pl.BlockSpec(memory_space=pltpu.VMEM)
SMEM = pl.BlockSpec(memory_space=pltpu.SMEM)
ANY = pl.BlockSpec(memory_space=pl.ANY)
DMA = pltpu.SemaphoreType.DMA
H = 128
T = 128
KT = 12
FB = 32
CB = 20
NF = FB * T
NC = CB * T
SEND = 256
HALO = 4 * SEND
QUAD = 4 * T
UNROLL = 16
GATHER = 32
ORDER = (2, 3, 0, 1)
NN = (((1,), (0,)), ((), ()))
NT = (((1,), (1,)), ((), ()))
TN = (((0,), (0,)), ((), ()))


def dot(a, b, how=NN):
    return lax.dot_general(a, b, how, preferred_element_type=F32)


def shape(dims, dtype):
    return jax.ShapeDtypeStruct(dims, dtype)


def params(mib=56, **more):
    return pltpu.CompilerParams(vmem_limit_bytes=mib * 2**20, **more)


def neighbour(me, n, offset):
    return lax.rem(me + (offset + n), n)


def greet(me, n):
    barrier = pltpu.get_barrier_semaphore()
    for offset in OFFSETS:
        pl.semaphore_signal(
            barrier, inc=1, device_id=(neighbour(me, n, offset),), device_id_type=MESH
        )
    return barrier


def remote(src, dst, send_sem, recv_sem, target):
    return pltpu.make_async_remote_copy(
        src_ref=src,
        dst_ref=dst,
        send_sem=send_sem,
        recv_sem=recv_sem,
        device_id=(target,),
        device_id_type=MESH,
    )


def index_copies(pairs, sem):
    copies = []
    for src, dst in pairs:
        width = src.shape[2]
        for j in range(src.shape[1]):
            copies.append((src.at[0, j], dst.at[pl.ds(j * width, width)]))
    return [pltpu.make_async_copy(a, b, sem.at[i]) for i, (a, b) in enumerate(copies)]


def loop(count, body, unroll=1):
    def step(i, carry):
        body(i)
        return carry

    lax.fori_loop(0, count, step, 0, unroll=unroll)


def gather_rows(index, first, source, target, count, step=1, shift=0):
    def body(i):
        base = pl.multiple_of(i * GATHER, GATHER)
        rows = [
            source[pl.ds(index[first + base + u] * step + shift, 1), :] for u in range(GATHER)
        ]
        for u in range(GATHER):
            target[pl.ds(base + u, 1), :] = rows[u]

    loop(count // GATHER, body)


def block_row(tiles, columns, blocks, b):
    lhs = jnp.concatenate([tiles[b, k] for k in range(KT)], axis=1)
    rhs = jnp.concatenate([blocks[columns[k, 0, b]] for k in range(KT)], axis=0)
    return dot(lhs, rhs)


def spread_row(tiles, columns, grads_t, b, total):
    for k in range(KT):
        c = columns[k, 0, b]
        total[c] = total[c] + dot(grads_t, tiles[b, k])


def tile_copies(source, buffer, sem, count):
    size = source.shape[0] // count
    return [
        pltpu.make_async_copy(
            source.at[pl.ds(i * size, size)], buffer.at[pl.ds(i * size, size)], sem.at[i]
        )
        for i in range(count)
    ]


AHEAD = 2


def start_tiles(source, buffer, sem, i, size):
    pltpu.make_async_copy(
        source.at[pl.ds(i * size, size)], buffer.at[pl.ds(i * size, size)], sem.at[i]
    ).start()


def next_tiles(source, buffer, sem, i, size):
    wait_tiles(source, buffer, sem, i, size)

    @pl.when(i + AHEAD < source.shape[0] // size)
    def _():
        start_tiles(source, buffer, sem, i + AHEAD, size)


def wait_tiles(source, buffer, sem, i, size):
    pltpu.make_async_copy(
        source.at[pl.ds(i * size, size)], buffer.at[pl.ds(i * size, size)], sem.at[i]
    ).wait()


def loads(pairs, sem):
    return [pltpu.make_async_copy(src, dst, sem.at[i]) for i, (src, dst) in enumerate(pairs)]


def lane_row(index):
    return jnp.concatenate([index[0, j : j + 1, :] for j in range(4)], axis=1)


def returned_rows(named, arrived, base, count):
    row = lax.broadcasted_iota(I32, (count, HALO), 0)
    chosen = jnp.where(jnp.broadcast_to(named - base, (count, HALO)) == row, 1.0, 0.0).astype(BF16)
    return dot(chosen, arrived)


WIDE = 512
ROWS = 48


def placed(rows, numbers):
    high, low = rows // T, rows % T
    at = jnp.broadcast_to(high, (ROWS, WIDE)) == lax.broadcasted_iota(I32, (ROWS, WIDE), 0)
    parts = [
        jnp.where(at, jnp.broadcast_to(part.astype(F32), (ROWS, WIDE)), 0.0).astype(BF16)
        for part in (numbers // 64, numbers % 64)
    ]
    lanes = jnp.where(
        jnp.broadcast_to(low, (T, WIDE)) == lax.broadcasted_iota(I32, (T, WIDE), 0), 1.0, 0.0
    ).astype(BF16)
    return dot(jnp.concatenate(parts, axis=0), lanes, NT)


def whole(tables):
    return (tables[:ROWS] * 64.0 + tables[ROWS:]).astype(I32)


def sources(members, pair_send, live):
    nowhere = ROWS * T - 1
    cells = jnp.zeros((2 * ROWS, T), F32)
    for j in range(2):
        for k in range(NC // WIDE):
            cell = lax.broadcasted_iota(I32, (1, WIDE), 1) + k * WIDE
            row = members[0, j : j + 1, k * WIDE : (k + 1) * WIDE]
            cells = cells + placed(jnp.where(cell < live, row, nowhere), cell + 1)
    slots = jnp.zeros((2 * ROWS, T), F32)
    sent = lane_row(pair_send)
    for k in range(HALO // WIDE):
        slot = lax.broadcasted_iota(I32, (1, WIDE), 1) + (NC + k * WIDE)
        slots = slots + placed(sent[:, k * WIDE : (k + 1) * WIDE], slot + 1)
    cells, slots = whole(cells), whole(slots)
    found = jnp.where(cells > 0, cells, jnp.where(slots > 0, slots, NC + HALO + 1)) - 1
    return jnp.minimum(found, NC + HALO)


def forward_kernel(
    n,
    weights,
    member_rows,
    pair_rows,
    count_hbm,
    values_hbm,
    cot_hbm,
    columns_hbm,
    fine_halo,
    coarse_halo,
    pair_send,
    members,
    tiles,
    h1_hbm,
    gate_hbm,
    slope_hbm,
    halo_hbm,
    z0_hbm,
    z0_halo_hbm,
    dz1_hbm,
    table,
    values,
    cot,
    h1,
    gates,
    slopes,
    z0_rows,
    dz1_rows,
    buf,
    ext,
    rows32,
    pairs,
    cells,
    stage,
    send_fine,
    recv_fine,
    send_cot,
    recv_cot,
    send_pair,
    recv_pair,
    send_coarse,
    recv_coarse,
    s_fine,
    s_coarse,
    s_pair,
    s_members,
    columns,
    count,
    load_sem,
    store_sem,
    tile_sem,
    index_sem,
    send_sem,
    recv_sem,
):
    me = lax.axis_index("dom")
    barrier = greet(me, n)
    taken = loads([(values_hbm, values), (cot_hbm, cot)], load_sem)
    index = index_copies(
        [(fine_halo, s_fine), (coarse_halo, s_coarse), (pair_send, s_pair), (members, s_members)],
        index_sem,
    )
    index.append(pltpu.make_async_copy(columns_hbm, columns, index_sem.at[14]))
    index.append(pltpu.make_async_copy(count_hbm, count, index_sem.at[15]))
    for copy in taken[:1] + index:
        copy.start()
    taken[0].wait()
    taken[1].start()
    for copy in tile_copies(tiles, buf, tile_sem, 8):
        copy.start()

    def widen(i):
        at = pl.ds(i * QUAD, QUAD)
        rows32[at, :] = values[at, :].astype(F32)

    loop(NF // QUAD, widen)
    for copy in index:
        copy.wait()
    targets = [neighbour(me, n, offset) for offset in OFFSETS]

    def exchange(index, source, sent, received, first, step=1, shift=0, ready=None):
        copies = [None] * 4
        for j in ORDER:
            gather_rows(index, j * SEND, source, stage, SEND, step, shift)
            sent[j] = stage[...].astype(BF16)
            if ready is not None and j == ORDER[0]:
                pl.semaphore_wait(ready, 4)
            copy = remote(
                sent.at[j],
                received.at[j],
                send_sem.at[first + j],
                recv_sem.at[first + j],
                targets[j],
            )
            copy.start()
            copies[j] = copy
        return copies

    fine = exchange(s_fine, rows32, send_fine, recv_fine, 0, ready=barrier)

    def project(i):
        at = pl.ds(i * QUAD, QUAD)
        ext[pl.ds(i * 4, 4)] = dot(values[at, :], weights[0]).astype(BF16).reshape(4, T, H)

    loop(NF // QUAD, project)
    taken[1].wait()

    def place_cot(i):
        pairs[pl.ds(i * 2 * QUAD + 1, QUAD, stride=2), :] = cot[pl.ds(i * QUAD, QUAD), :].astype(F32)

    loop(NF // QUAD, place_cot)
    paired_cot = exchange(s_pair, pairs, send_cot, recv_cot, 12, 2, 1)
    table[...] = sources(member_rows, pair_rows, count[0])
    pairs[pl.ds(2 * NF, HALO, stride=2), :] = jnp.zeros((HALO, H), F32)
    for j in range(4):
        fine[j].wait()
        ext[pl.ds(FB + 2 * j, 2)] = dot(recv_fine[j], weights[0]).astype(BF16).reshape(2, T, H)

    def level(i):
        wait_tiles(tiles, buf, tile_sem, i, 4)
        parts = []
        for q in range(4):
            b = i * 4 + q
            parts.append(block_row(buf, columns, ext, b))
        summed = jnp.concatenate(parts, axis=0)
        sigma = jax.nn.sigmoid(summed)
        gate = (summed * sigma).astype(BF16)
        at = pl.ds(i * QUAD, QUAD)
        gates[at, :] = gate
        slopes[at, :] = (sigma * (1.0 + summed * (1.0 - sigma))).astype(BF16)
        out = (values[at, :].astype(F32) + dot(gate, weights[1])).astype(BF16)
        h1[at, :] = out
        pairs[pl.ds(i * 2 * QUAD, QUAD, stride=2), :] = out.astype(F32)

    loop(8, level)
    paired = exchange(s_pair, pairs, send_pair, recv_pair, 4, 2, 0)
    outs = [(h1, h1_hbm), (gates, gate_hbm), (slopes, slope_hbm), (recv_fine, halo_hbm)]
    stored = loads(outs, store_sem)
    for copy in stored:
        copy.start()
    for j in range(4):
        paired_cot[j].wait()
        pairs[pl.ds(2 * (NF + j * SEND) + 1, SEND, stride=2), :] = recv_cot[j].astype(F32)

    def pool(i):
        base = pl.multiple_of(i * 2 * GATHER, 2 * GATHER)
        for half in range(0, 2 * GATHER, GATHER):
            at = range(half, half + GATHER)
            first = [pairs[pl.ds(s_members[base + u] * 2, 2), :] for u in at]
            second = [pairs[pl.ds(s_members[NC + base + u] * 2, 2), :] for u in at]
            for u in at:
                cells[pl.ds((base + u) * 2, 2), :] = first[u - half] + second[u - half]

    loop(NC // (2 * GATHER), pool)
    live = count[0]
    for copy in paired:
        copy.wait()
    named = jnp.concatenate([table[FB + t : FB + t + 1, :] for t in range(8)], axis=1)

    def pooled(i):
        at = pl.ds(i * QUAD, QUAD)
        row = lax.broadcasted_iota(I32, (QUAD, H), 0) + i * QUAD
        received = jnp.concatenate(
            [
                returned_rows(named, recv_pair[...].reshape(HALO, H), i * QUAD + q * SEND, SEND)
                for q in range(2)
            ],
            axis=0,
        )
        z0 = cells[pl.ds(i * 2 * QUAD, QUAD, stride=2), :] + received
        z0 = jnp.where(row < live, z0, 0.0).astype(BF16)
        z0_rows[at, :] = z0
        rows32[at, :] = z0.astype(F32)

    loop(NC // QUAD, pooled)
    coarse = exchange(s_coarse, rows32, send_coarse, recv_coarse, 8)
    stored += loads([(z0_rows, z0_hbm)], store_sem.at[pl.ds(4, 1)])
    stored[-1].start()

    def pooled_cot(i):
        at = pl.ds(i * QUAD, QUAD)
        row = lax.broadcasted_iota(I32, (QUAD, H), 0) + i * QUAD
        dz1_rows[at, :] = jnp.where(
            row < live, cells[pl.ds(i * 2 * QUAD + 1, QUAD, stride=2), :], 0.0
        ).astype(BF16)

    loop(NC // QUAD, pooled_cot)
    stored += loads([(dz1_rows, dz1_hbm)], store_sem.at[pl.ds(5, 1)])
    stored[-1].start()
    for copy in coarse:
        copy.wait()
    stored += loads([(recv_coarse, z0_halo_hbm)], store_sem.at[pl.ds(6, 1)])
    stored[-1].start()
    for copy in stored:
        copy.wait()


def forward(n, weights, count, values, cot, columns, fine_halo, coarse_halo, pair_send, members, tiles):
    return pl.pallas_call(
        functools.partial(forward_kernel, n),
        name="forward",
        out_shape=[
            shape((NF, H), BF16),
            shape((NF, H), BF16),
            shape((NF, H), BF16),
            shape((4, SEND, H), BF16),
            shape((NC, H), BF16),
            shape((4, SEND, H), BF16),
            shape((NC, H), BF16),
            shape((ROWS, T), I32),
        ],
        in_specs=[VMEM] * 3 + [ANY] * 9,
        out_specs=[ANY] * 7 + [VMEM],
        scratch_shapes=[pltpu.VMEM((NF, H), BF16)] * 5
        + [pltpu.VMEM((NC, H), BF16)] * 2
        + [
            pltpu.VMEM((FB, KT, T, T), BF16),
            pltpu.VMEM((FB + 8, T, H), BF16),
            pltpu.VMEM((NF, H), F32),
            pltpu.VMEM((2 * (NF + HALO), H), F32),
            pltpu.VMEM((2 * NC, H), F32),
            pltpu.VMEM((SEND, H), F32),
        ]
        + [pltpu.VMEM((4, SEND, H), BF16)] * 8
        + [
            pltpu.SMEM((HALO,), I32),
            pltpu.SMEM((HALO,), I32),
            pltpu.SMEM((HALO,), I32),
            pltpu.SMEM((2 * NC,), I32),
            pltpu.SMEM((KT, 1, FB), I32),
            pltpu.SMEM((1,), I32),
            DMA((2,)),
            DMA((7,)),
            DMA((8,)),
            DMA((16,)),
            DMA((16,)),
            DMA((16,)),
        ],
        compiler_params=params(collective_id=0, has_side_effects=True),
    )(
        weights,
        members,
        pair_send,
        count,
        values,
        cot,
        columns,
        fine_halo,
        coarse_halo,
        pair_send,
        members,
        tiles,
    )


def rows_out(total, blocks, own_values, halo_values, own, own_hbm, sem, halo_ref, message_ref):
    def place(c):
        part = total[c]
        at = pl.ds(c * T, T)
        own[at, :] = jnp.transpose(part)
        message_ref[...] += dot(part.astype(BF16), own_values[at, :])

    def halo(c):
        part = total[blocks + c]
        halo_ref[pl.ds(c * T, T), :] = jnp.transpose(part).astype(BF16)
        message_ref[...] += dot(part.astype(BF16), halo_values[c // 2, pl.ds(c % 2 * T, T), :])

    message_ref[...] = jnp.zeros_like(message_ref)
    quarter = blocks // 4
    copies = []
    for part in range(4):
        loop(quarter, lambda c: place(part * quarter + c), quarter)
        at = pl.ds(part * quarter * T, quarter * T)
        copies.append(pltpu.make_async_copy(own.at[at], own_hbm.at[at], sem.at[part]))
        copies[-1].start()
    loop(8, halo, 8)
    message_ref[...] = jnp.transpose(message_ref[...])
    for copy in copies:
        copy.wait()


def coarse_kernel(
    z0,
    z0_halo,
    dz1,
    weights,
    columns_hbm,
    tiles,
    z1_out,
    dm_hbm,
    piece_out,
    message_out,
    update_out,
    dm,
    dm_sem,
    buf,
    ext,
    gates,
    total,
    columns,
    tile_sem,
    index_sem,
):
    index = pltpu.make_async_copy(columns_hbm, columns, index_sem)
    index.start()
    for first in range(AHEAD):
        start_tiles(tiles, buf, tile_sem, first, 4)

    def project(i):
        part = z0[pl.ds(i * QUAD, QUAD), :]
        ext[pl.ds(i * 4, 4)] = dot(part, weights[2]).astype(BF16).reshape(4, T, H)

    loop(CB // 4, project)
    ext[pl.ds(CB, 8)] = dot(z0_halo[...].reshape(HALO, H), weights[2]).astype(BF16).reshape(8, T, H)
    total[...] = jnp.zeros_like(total)
    index.wait()

    def level(i):
        next_tiles(tiles, buf, tile_sem, i, 4)
        parts = []
        for q in range(4):
            b = i * 4 + q
            parts.append(block_row(buf, columns, ext, b))
        summed = jnp.concatenate(parts, axis=0)
        sigma = jax.nn.sigmoid(summed)
        gate = (summed * sigma).astype(BF16)
        at = pl.ds(i * QUAD, QUAD)
        gates[at, :] = gate
        z1_out[at, :] = (z0[at, :].astype(F32) + dot(gate, weights[3])).astype(BF16)
        slope = sigma * (1.0 + summed * (1.0 - sigma))
        grads = (dot(dz1[at, :], weights[3], NT) * slope).astype(BF16)
        for q in range(4):
            b = i * 4 + q
            grads_t = jnp.transpose(grads[q * T : (q + 1) * T, :])
            spread_row(buf, columns, grads_t, b, total)

    loop(CB // 4, level)
    update_out[...] = dot(gates[...], dz1[...], TN)
    rows_out(total, CB, z0, z0_halo, dm, dm_hbm, dm_sem, piece_out, message_out)


def coarse_level(z0, z0_halo, dz1, weights, columns, tiles):
    return pl.pallas_call(
        coarse_kernel,
        name="coarse_level",
        out_shape=[
            shape((NC, H), BF16),
            shape((NC, H), F32),
            shape((HALO, H), BF16),
            shape((H, H), F32),
            shape((H, H), F32),
        ],
        in_specs=[VMEM, VMEM, VMEM, VMEM, ANY, ANY],
        out_specs=[VMEM, ANY, VMEM, VMEM, VMEM],
        scratch_shapes=[
            pltpu.VMEM((NC, H), F32),
            DMA((4,)),
            pltpu.VMEM((CB, KT, T, T), BF16),
            pltpu.VMEM((CB + 8, T, H), BF16),
            pltpu.VMEM((NC, H), BF16),
            pltpu.VMEM((CB + 8, T, H), F32),
            pltpu.SMEM((KT, 1, CB), I32),
            DMA((5,)),
            DMA,
        ],
        compiler_params=params(),
    )(z0, z0_halo, dz1, weights, columns, tiles)


def gather_block(index, block, source, target, first, width=2, shift=0):
    for g in range(T // UNROLL):
        rows = [
            source[pl.ds(index[block, g * UNROLL + u] * 2 + shift, width), :]
            for u in range(UNROLL)
        ]
        for u in range(UNROLL):
            target[pl.ds((first + g * UNROLL + u) * width, width), :] = rows[u]


NEAR = 8
SIDE = 4
SUM_SEMS = 2 * (NEAR - 1 + SIDE - 1)


class GroupSum:
    def __init__(self, me, grads, near, sides, total, send, recv):
        self.grads, self.near, self.sides, self.total = grads, near, sides, total
        self.send, self.recv = send, recv
        self.rank = me % NEAR
        base = me - self.rank
        self.close = [base + (self.rank + s) % NEAR for s in range(1, NEAR)]
        z, y = me // NEAR % SIDE, me // (NEAR * SIDE)
        self.place = (z, y)
        self.rows = (
            [me + ((z + s) % SIDE - z) * NEAR for s in range(1, SIDE)],
            [me + ((y + s) % SIDE - y) * NEAR * SIDE for s in range(1, SIDE)],
        )
        self.size = near.shape[1]
        self.copies = []

    def greet(self, barrier):
        targets = self.close + self.rows[0] + self.rows[1]
        for target in targets:
            pl.semaphore_signal(barrier, inc=1, device_id=(target,), device_id_type=MESH)
        return len(targets)

    def launch(self, first, moves):
        self.copies = [
            remote(src, dst, self.send.at[first + s], self.recv.at[first + s], target)
            for s, (src, dst, target) in enumerate(moves)
        ]
        for copy in self.copies:
            copy.start()

    def wait(self):
        for copy in self.copies:
            copy.wait()

    def to_near(self):
        size = self.size
        self.launch(
            0,
            [
                (
                    self.grads.at[pl.ds((self.rank + s + 1) % NEAR * size, size)],
                    self.near.at[s],
                    self.close[s],
                )
                for s in range(NEAR - 1)
            ],
        )

    def along(self, side, summed):
        held, place = self.sides[side], self.place[side]
        held[place] = summed
        self.launch(
            NEAR - 1 + side * (SIDE - 1),
            [(held.at[place], held.at[place], target) for target in self.rows[side]],
        )

    def to_z(self):
        self.wait()
        summed = self.grads[pl.ds(self.rank * self.size, self.size), :]
        for s in range(NEAR - 1):
            summed = summed + self.near[s]
        self.along(0, summed)

    def added(self, side):
        self.wait()
        held = self.sides[side]
        return (held[0] + held[1]) + (held[2] + held[3])

    def to_y(self):
        self.along(1, self.added(0))

    def to_all(self):
        mine = pl.ds(self.rank * self.size, self.size)
        self.total[mine, :] = self.added(1)
        self.launch(
            NEAR - 1 + 2 * (SIDE - 1),
            [(self.total.at[mine], self.total.at[mine], target) for target in self.close],
        )


def sum_scratch():
    size = 2 * H // NEAR
    return [
        pltpu.VMEM((2 * H, H), F32),
        pltpu.VMEM((NEAR - 1, size, H), F32),
        pltpu.VMEM((SIDE, size, H), F32),
        pltpu.VMEM((SIDE, size, H), F32),
        pltpu.VMEM((2 * H, H), F32),
        DMA((SUM_SEMS,)),
        DMA((SUM_SEMS,)),
    ]


def coarse_back_kernel(
    n,
    weights,
    coarse_halo,
    m1,
    u1,
    table,
    pieces,
    dm,
    dz1_hbm,
    z1_hbm,
    h1_hbm,
    cot_hbm,
    gate_hbm,
    slope_hbm,
    result_hbm,
    low_hbm,
    grads_hbm,
    update_out,
    total_out,
    result_out,
    low_out,
    grads_out,
    arrived,
    rows,
    dz1,
    z1,
    h1,
    cot,
    gate,
    slope,
    cells,
    stage,
    even,
    odd,
    send_out,
    recv_out,
    send_away,
    recv_away,
    source,
    load_sem,
    store_sem,
    index_sem,
    send_sem,
    recv_sem,
    grads1,
    *sum_refs,
):
    me = lax.axis_index("dom")
    barrier = greet(me, n)
    group = GroupSum(me, grads1, sum_refs[0], sum_refs[1:3], *sum_refs[3:])
    partners = 4 + group.greet(barrier)
    early = loads([(z1_hbm, z1), (dm, rows), (dz1_hbm, dz1)], load_sem)
    later = loads(
        [(h1_hbm, h1), (cot_hbm, cot), (gate_hbm, gate), (slope_hbm, slope)],
        load_sem.at[pl.ds(3, 4)],
    )
    for copy in early:
        copy.start()
    targets = [neighbour(me, n, -offset) for offset in OFFSETS]
    grads1[:H, :] = m1[...]
    grads1[H:, :] = u1[...]
    index = pltpu.make_async_copy(table, source, index_sem)
    index.start()
    pl.semaphore_wait(barrier, partners)
    back = [
        remote(
            pieces.at[pl.ds(j * SEND, SEND)],
            arrived.at[pl.ds(j * SEND, SEND)],
            send_sem.at[j],
            recv_sem.at[j],
            targets[j],
        )
        for j in ORDER
    ]
    for copy in back:
        copy.start()
    group.to_near()
    for copy in early:
        copy.wait()
    for copy in later:
        copy.start()
    cells[pl.ds(2 * (NC + HALO), 16), :] = jnp.zeros((16, H), F32)
    update_out[...] = jnp.zeros_like(update_out)
    named = lane_row(coarse_halo)

    def place(i):
        cells[pl.ds(i * 2 * QUAD, QUAD, stride=2), :] = z1[pl.ds(i * QUAD, QUAD), :].astype(F32)

    loop(NC // QUAD, place)

    def exchange_away(shift, sent, received, first):
        copies = [None] * 4
        for j in ORDER:
            loop(
                2,
                lambda t: gather_block(source, FB + 2 * j + t, cells, stage, t * T, 1, shift),
            )
            sent[j] = stage[...].astype(BF16)
            copy = remote(
                sent.at[j],
                received.at[j],
                send_sem.at[first + j],
                recv_sem.at[first + j],
                targets[j],
            )
            copy.start()
            copies[j] = copy
        return copies

    index.wait()
    away_out = exchange_away(0, send_out, recv_out, 8)
    group.to_z()
    for copy in back:
        copy.wait()

    def retract(i):
        at = pl.ds(i * QUAD, QUAD)
        parts = [
            rows[pl.ds(i * QUAD + q * SEND, SEND), :]
            + returned_rows(named, arrived[...], i * QUAD + q * SEND, SEND)
            for q in range(2)
        ]
        low = jnp.concatenate(parts, axis=0).astype(BF16)
        cells[pl.ds(i * 2 * QUAD + 1, QUAD, stride=2), :] = dz1[at, :].astype(F32) + dot(
            low, weights[2], NT
        )

    loop(NC // QUAD, retract)
    away = exchange_away(1, send_away, recv_away, 4)
    group.to_y()
    for copy in later:
        copy.wait()
    for shift, copies, received in ((0, away_out, recv_out), (1, away, recv_away)):
        for j in range(4):
            copies[j].wait()
            cells[pl.ds(2 * (NC + j * SEND) + shift, SEND, stride=2), :] = received[j].astype(F32)

    def lift(b, lifted):
        at = pl.ds(b * T, T)
        result_out[at, :] = (h1[at, :].astype(F32) + lifted[pl.ds(0, T, stride=2), :]).astype(BF16)
        low = (cot[at, :].astype(F32) + lifted[pl.ds(1, T, stride=2), :]).astype(BF16)
        low_out[at, :] = low
        update_out[...] += dot(gate[at, :], low, TN)
        grads_out[at, :] = (dot(low, weights[1], NT) * slope[at, :].astype(F32)).astype(BF16)

    def lift_two(i):
        gather_block(source, 2 * i + 1, cells, odd, 0)
        lift(2 * i, even)
        gather_block(source, (2 * i + 2) % FB, cells, even, 0)
        lift(2 * i + 1, odd)

    group.to_all()
    gather_block(source, 0, cells, even, 0)
    half = FB // 4
    loop(half, lift_two)
    outs = ((result_out, result_hbm), (low_out, low_hbm), (grads_out, grads_hbm))

    def store(first, sem):
        at = pl.ds(first, NF // 2)
        copies = loads([(src.at[at], dst.at[at]) for src, dst in outs], sem)
        for copy in copies:
            copy.start()
        return copies

    stored = store(0, store_sem.at[pl.ds(0, 3)])
    loop(half, lambda i: lift_two(i + half))
    stored += store(NF // 2, store_sem.at[pl.ds(3, 3)])
    group.wait()
    total_out[...] = group.total[...]
    for copy in stored:
        copy.wait()


def coarse_back(
    n, number, weights, coarse_halo, m1, u1, table, pieces, dm, dz1, z1, h1, cot, gate, slope
):
    return pl.pallas_call(
        functools.partial(coarse_back_kernel, n),
        name="coarse_back",
        out_shape=[
            shape((NF, H), BF16),
            shape((NF, H), BF16),
            shape((NF, H), BF16),
            shape((H, H), F32),
            shape((2 * H, H), F32),
        ],
        in_specs=[VMEM] * 4 + [ANY] * 9,
        out_specs=[ANY] * 3 + [VMEM] * 2,
        scratch_shapes=[pltpu.VMEM((NF, H), BF16)] * 3
        + [
            pltpu.VMEM((HALO, H), BF16),
            pltpu.VMEM((NC, H), F32),
            pltpu.VMEM((NC, H), BF16),
            pltpu.VMEM((NC, H), BF16),
        ]
        + [pltpu.VMEM((NF, H), BF16)] * 4
        + [
            pltpu.VMEM((2 * (NC + HALO) + 16, H), F32),
            pltpu.VMEM((SEND, H), F32),
            pltpu.VMEM((2 * T, H), F32),
            pltpu.VMEM((2 * T, H), F32),
        ]
        + [pltpu.VMEM((4, SEND, H), BF16)] * 4
        + [
            pltpu.SMEM((ROWS, T), I32),
            DMA((7,)),
            DMA((6,)),
            DMA,
            DMA((12,)),
            DMA((12,)),
        ]
        + sum_scratch(),
        compiler_params=params(collective_id=number, has_side_effects=True),
    )(
        weights,
        coarse_halo,
        m1,
        u1,
        table,
        pieces,
        dm,
        dz1,
        z1,
        h1,
        cot,
        gate,
        slope,
    )


def fine_kernel(
    grads_hbm,
    values_hbm,
    halo_hbm,
    columns_hbm,
    tiles,
    result_in,
    dm_hbm,
    piece_out,
    message_out,
    result_out,
    grads,
    values,
    halo,
    result,
    dm,
    buf,
    total,
    columns,
    load_sem,
    store_sem,
    tile_sem,
):
    first = loads([(columns_hbm, columns), (grads_hbm, grads)], load_sem)
    for copy in first:
        copy.start()
    for ahead in range(AHEAD):
        start_tiles(tiles, buf, tile_sem, ahead, 4)
    total[...] = jnp.zeros_like(total)
    for copy in first:
        copy.wait()
    later = loads(
        [(values_hbm, values), (halo_hbm, halo), (result_in, result)], load_sem.at[pl.ds(2, 3)]
    )

    def level(i):
        next_tiles(tiles, buf, tile_sem, i, 4)
        for q in range(4):
            b = i * 4 + q
            spread_row(buf, columns, jnp.transpose(grads[pl.ds(b * T, T), :]), b, total)

    loop(2, level)
    for copy in later:
        copy.start()
    loop(4, lambda i: level(i + 2))
    for copy in later:
        copy.wait()
    passed = pltpu.make_async_copy(result, result_out, store_sem.at[4])
    passed.start()
    loop(2, lambda i: level(i + 6))
    rows_out(total, FB, values, halo, dm, dm_hbm, store_sem, piece_out, message_out)
    passed.wait()


def fine_spread(grads, values, halo, columns, tiles, result):
    return pl.pallas_call(
        fine_kernel,
        name="fine_spread",
        out_shape=[
            shape((NF, H), F32),
            shape((HALO, H), BF16),
            shape((H, H), F32),
            shape((NF, H), BF16),
        ],
        in_specs=[ANY] * 6,
        out_specs=[ANY, VMEM, VMEM, ANY],
        scratch_shapes=[
            pltpu.VMEM((NF, H), BF16),
            pltpu.VMEM((NF, H), BF16),
            pltpu.VMEM((4, SEND, H), BF16),
            pltpu.VMEM((NF, H), BF16),
            pltpu.VMEM((NF, H), F32),
            pltpu.VMEM((FB, KT, T, T), BF16),
            pltpu.VMEM((FB + 8, T, H), F32),
            pltpu.SMEM((KT, 1, FB), I32),
            DMA((5,)),
            DMA((5,)),
            DMA((8,)),
        ],
        compiler_params=params(),
    )(grads, values, halo, columns, tiles, result)


def fine_back_kernel(
    n,
    weights,
    fine_halo,
    m0,
    u0,
    pieces,
    dm,
    low_hbm,
    grad_hbm,
    total_out,
    arrived,
    rows,
    low,
    grad_out,
    load_sem,
    store_sem,
    send_sem,
    recv_sem,
    grads0,
    *sum_refs,
):
    me = lax.axis_index("dom")
    barrier = greet(me, n)
    group = GroupSum(me, grads0, sum_refs[0], sum_refs[1:3], *sum_refs[3:])
    partners = 4 + group.greet(barrier)
    copies = loads([(dm, rows), (low_hbm, low)], load_sem)
    for copy in copies:
        copy.start()
    grads0[:H, :] = m0[...]
    grads0[H:, :] = u0[...]
    named = lane_row(fine_halo)
    pl.semaphore_wait(barrier, partners)
    group.to_near()
    back = [
        remote(
            pieces.at[pl.ds(j * SEND, SEND)],
            arrived.at[pl.ds(j * SEND, SEND)],
            send_sem.at[j],
            recv_sem.at[j],
            neighbour(me, n, -OFFSETS[j]),
        )
        for j in ORDER
    ]
    for copy in back:
        copy.start()
    group.to_z()
    for copy in copies + back:
        copy.wait()

    def retract(i):
        at = pl.ds(i * QUAD, QUAD)
        parts = [
            rows[pl.ds(i * QUAD + q * SEND, SEND), :]
            + returned_rows(named, arrived[...], i * QUAD + q * SEND, SEND)
            for q in range(2)
        ]
        part = jnp.concatenate(parts, axis=0).astype(BF16)
        grad_out[at, :] = (low[at, :].astype(F32) + dot(part, weights[0], NT)).astype(BF16)

    loop(3, retract)
    group.to_y()
    loop(5, lambda i: retract(i + 3))
    group.to_all()
    stored = pltpu.make_async_copy(grad_out, grad_hbm, store_sem)
    stored.start()
    group.wait()
    total_out[...] = group.total[...]
    stored.wait()


def fine_back(n, number, weights, fine_halo, m0, u0, pieces, dm, low):
    return pl.pallas_call(
        functools.partial(fine_back_kernel, n),
        name="fine_back",
        out_shape=[shape((NF, H), BF16), shape((2 * H, H), F32)],
        in_specs=[VMEM] * 4 + [ANY] * 3,
        out_specs=[ANY, VMEM],
        scratch_shapes=[
            pltpu.VMEM((HALO, H), BF16),
            pltpu.VMEM((NF, H), F32),
            pltpu.VMEM((NF, H), BF16),
            pltpu.VMEM((NF, H), BF16),
            DMA((2,)),
            DMA,
            DMA((4,)),
            DMA((4,)),
        ]
        + sum_scratch(),
        compiler_params=params(collective_id=number, has_side_effects=True),
    )(weights, fine_halo, m0, u0, pieces, dm, low)


def finish_kernel(grad, fine, coarse, grad_out, totals_out):
    grad_out[...] = grad[...]
    totals_out[pl.ds(0, 2)] = fine[...].reshape(2, H, H)
    totals_out[pl.ds(2, 2)] = coarse[...].reshape(2, H, H)


def finish(grad, fine, coarse):
    return pl.pallas_call(
        finish_kernel,
        name="finish",
        out_shape=[shape(grad.shape, grad.dtype), shape((4, H, H), F32)],
        in_specs=[VMEM] * 3,
        out_specs=[VMEM] * 2,
        compiler_params=params(),
    )(grad, fine, coarse)


def per_device(
    n,
    features,
    cotangent,
    weights,
    fine_tiles,
    fine_columns,
    fine_halo,
    coarse_tiles,
    coarse_columns,
    coarse_halo,
    pair_send,
    members,
    coarse_count,
):
    fine_cols = jnp.transpose(fine_columns, (2, 0, 1))
    coarse_cols = jnp.transpose(coarse_columns, (2, 0, 1))
    h1, gate, slope, halo, z0, z0_halo, dz1, table = forward(
        n,
        weights,
        coarse_count,
        features,
        cotangent,
        fine_cols,
        fine_halo,
        coarse_halo,
        pair_send,
        members,
        fine_tiles,
    )
    z1, dm1, piece1, message1, update1 = coarse_level(
        z0, z0_halo, dz1, weights, coarse_cols, coarse_tiles
    )
    result, low, grads, update0, totals1 = coarse_back(
        n,
        1,
        weights,
        coarse_halo,
        message1,
        update1,
        table,
        piece1,
        dm1,
        dz1,
        z1,
        h1,
        cotangent,
        gate,
        slope,
    )
    dm0, piece0, message0, result = fine_spread(
        grads, features, halo, fine_cols, fine_tiles, result
    )
    grad_features, totals0 = fine_back(
        n, 2, weights, fine_halo, message0, update0, piece0, dm0, low
    )
    grad_features, totals = finish(grad_features, totals0, totals1)
    return result, grad_features, totals


def solution(mesh):
    n = mesh.shape["dom"]
    placed = (
        P("dom", None),
        P("dom", None),
        P(),
        P("dom", None, None, None),
        P("dom", None, None),
        P("dom", None, None),
        P("dom", None, None, None),
        P("dom", None, None),
        P("dom", None, None),
        P("dom", None, None),
        P("dom", None, None),
        P("dom"),
    )
    return jax.shard_map(
        functools.partial(per_device, n),
        mesh=mesh,
        in_specs=placed,
        out_specs=(P("dom", None), P("dom", None), P()),
        check_vma=False,
    )
```
